32 devices in a mesh: gx: 4 (over y, x), gy: 8 (over z, core).
Axes of the slice: x: 2, y: 2, z: 4, core: 2. Of those that a mesh axis runs over, the one named last changes fastest.
Arguments:
- adjoint_e: bfloat16 [3, 128, 512, 128], P(None, 'gx', 'gy'), may hold values from -6 to 6
- adjoint_h: bfloat16 [3, 128, 512, 128], P(None, 'gx', 'gy'), may hold values from -6 to 6
- material: int32 [128, 512, 128], P('gx', 'gy'), may hold values from 0 to 3
- inv_eps: float32 [4], replicated, may hold values from 0.08 to 1
- forward_design: bfloat16 [3, 128, 512, 128], P(None, 'gx', 'gy'), may hold values from -6 to 6
- cell_slot: int32 [128, 512], P('gx', 'gy'), may hold values from 0 to 511, as said below
- tile_pillars: int32 [4, 8, 512], replicated, may hold values from -1 to 16383, as said below
- pillar_rank: int32 [16384], replicated, may hold values from 0 to 16383, as said below
Outputs:
- new_e: bfloat16 [3, 128, 512, 128], P(None, 'gx', 'gy')
- new_h: bfloat16 [3, 128, 512, 128], P(None, 'gx', 'gy')
- gradient: float32 [32, 16384], P(None, ('gx', 'gy'))
The draws below stay inside these ranges and needn't reach their ends.
Inputs may be any that keep to these rules, and one draw needn't show every extreme that they name: `cell_slot`: the cell's slot holds the id of the pillar that covers the cell. `tile_pillars`: pillars are rectangles of 2 or 3 cells along x and along y that tile the lateral grid and never cross a tile's border. The lx-th pillar along x and ly-th along y of tile (tx, ty), counted from the tile's low corner, has id (tx * 16 + lx) * 256 + ty * 32 + ly. Each tile lists every pillar in it exactly once, in no particular order, with -1 in unused slots; tile (0, 0) uses all 512 slots. `pillar_rank`: A permutation of the pillar ids; rank r is owned by device r // 512 of gx+gy. Of the 512 ids of one tile, exactly 16 have ranks owned by each device.
All inputs are finite; a program needn't handle non-finite values.
Results may differ from the reference program's by a relative error of at most 0.0049.
Values may be sent and summed in bfloat16 or wider, within the bound.
A program may use at most 128 MiB of HBM per device.

```python
import math
import jax
import jax.numpy as jnp
from jax import lax

CX = 32
CY = 64
NZ = 128
DZ = 128
DL = 32
NMAT = 4
NX = 128
NY = 512
KY = 256
P_SIZE = 16384
PT = 512


def axis_pillars(key, cells, tile_cells):
    segments = cells // tile_cells
    half = tile_cells // 2
    key_wide, key_turn = jax.random.split(key)
    wide_count = 2 * jax.random.randint(key_wide, (segments,), 0, tile_cells // 6 + 1)
    wide_count = wide_count.at[0].set(0).astype(jnp.int32)
    count = (half - wide_count // 2).astype(jnp.int32)
    turn = (jax.random.randint(key_turn, (segments,), 0, half) % count).astype(jnp.int32)
    steps = jnp.arange(half, dtype=jnp.int32)[None, :]
    shifted = steps + turn[:, None]
    wide = (shifted + 1) * wide_count[:, None] // count[:, None] - shifted * wide_count[:, None] // count[:, None]
    widths = jnp.where(steps < count[:, None], 2 + wide, 0).astype(jnp.int32)
    ends = jnp.cumsum(widths, axis=1)
    local_cells = jnp.arange(tile_cells, dtype=jnp.int32)
    local = jnp.sum((ends[:, None, :] <= local_cells[None, :, None]).astype(jnp.int32), axis=2)
    return (local.reshape(cells).astype(jnp.int32), count)


def pillar_lattice(key):
    base = jax.random.fold_in(key, 7)
    key_x, key_y, key_order = jax.random.split(base, 3)
    local_x, count_x = axis_pillars(key_x, NX, CX)
    local_y, count_y = axis_pillars(key_y, NY, CY)
    half_x = CX // 2
    half_y = CY // 2
    tiles_x = NX // CX
    tiles_y = NY // CY
    canon = jnp.arange(PT, dtype=jnp.int32)
    along_x = canon // half_y
    along_y = canon % half_y
    tile_x = jnp.arange(tiles_x, dtype=jnp.int32)[:, None, None]
    tile_y = jnp.arange(tiles_y, dtype=jnp.int32)[None, :, None]
    exists = (along_x[None, None, :] < count_x[:, None, None]) & (along_y[None, None, :] < count_y[None, :, None])
    ids = (tile_x * half_x + along_x[None, None, :]) * KY + tile_y * half_y + along_y[None, None, :]
    ids = jnp.where(exists, ids, -1).astype(jnp.int32)
    keys = jax.random.split(key_order, tiles_x * tiles_y)
    orders = jax.vmap(lambda one: jax.random.permutation(one, PT))(keys).reshape(tiles_x, tiles_y, PT).astype(jnp.int32)
    listed = jnp.take_along_axis(ids, orders, axis=2).astype(jnp.int32)
    inverse = jnp.argsort(orders, axis=2).astype(jnp.int32)
    cell_tx = (jnp.arange(NX) // CX).astype(jnp.int32)
    cell_ty = (jnp.arange(NY) // CY).astype(jnp.int32)
    position = local_x[:, None] * half_y + local_y[None, :]
    cell_slot = inverse[cell_tx[:, None], cell_ty[None, :], position]
    return (cell_slot.astype(jnp.int32), listed)


def draw_cell_slot(key, part):
    return pillar_lattice(key)[0]


def draw_tile_pillars(key, part):
    return pillar_lattice(key)[1]


def draw_pillar_rank(key, part):
    tiles_y = NY // CY
    tiles = NX // CX * tiles_y
    room = PT // tiles
    half_x = CX // 2
    half_y = CY // 2
    keys = jax.random.split(jax.random.fold_in(key, 11), tiles)
    perms = jax.vmap(lambda one: jax.random.permutation(one, PT))(keys).astype(jnp.int32)
    ident = jnp.arange(P_SIZE, dtype=jnp.int32)
    index_x = ident // KY
    index_y = ident % KY
    tile = index_x // half_x * tiles_y + index_y // half_y
    canon = index_x % half_x * half_y + index_y % half_y
    picked = perms[tile, canon]
    owner = (picked + tile) % tiles
    return (owner * PT + tile * room + picked // tiles).astype(jnp.int32)


def with_ends(entries, own_key, low, largest):
    dims = entries.shape
    place = [jax.random.randint(jax.random.fold_in(own_key, axis), (), 0, dims[axis]) for axis in range(len(dims))]
    entries = entries.at[tuple(place)].set(low)
    longest = dims.index(max(dims))
    place[longest] = (place[longest] + 1) % dims[longest]
    return entries.at[tuple(place)].set(largest)


def block_levels(rng, shape, shards, low, high):
    level, own = 1.0, jax.random.fold_in(rng, 6)
    for dim, blocks in shards:
        heights = jnp.exp(jax.random.uniform(jax.random.fold_in(own, dim), (blocks,), jnp.float32, low / len(shards), high / len(shards)))
        level = level * jnp.repeat(heights, shape[dim] // blocks).reshape([-1 if axis == dim else 1 for axis in range(len(shape))])
    return level


def centred(stream_key, extent, deviation, bound, cuts=(), held_as=jnp.bfloat16):
    array = deviation * jax.random.normal(stream_key, extent, jnp.float32)
    if cuts:
        array = array * block_levels(stream_key, extent, cuts, -0.22, 0.18)
    return jnp.clip(array, -bound, bound).astype(held_as)


def setup_inputs(seed: int = 0) -> dict:
    streams_of = jax.random.split(jax.random.key(seed), 9)
    return {
        "adjoint_e": centred(streams_of[0], (3, NX, NY, NZ), 1.0, 6.0, ((1, 4), (2, 8))),
        "adjoint_h": centred(streams_of[1], (3, NX, NY, NZ), 1.0, 6.0, ((1, 4), (2, 8))),
        "material": with_ends(jax.random.randint(streams_of[2], (NX, NY, NZ), 0, NMAT), jax.random.fold_in(streams_of[2], 1), 0, NMAT - 1).astype(jnp.int32),
        "inv_eps": jnp.clip(jnp.exp(jax.random.uniform(streams_of[3], (NMAT,), jnp.float32, math.log(0.08), math.log(1.0))), 0.08, 1.0),
        "forward_design": centred(streams_of[4], (3, NX, NY, DZ), 1.0, 6.0, ((1, 4), (2, 8))),
        "cell_slot": draw_cell_slot(jax.random.fold_in(streams_of[8], 71), 0),
        "tile_pillars": draw_tile_pillars(jax.random.fold_in(streams_of[8], 71), 0),
        "pillar_rank": draw_pillar_rank(jax.random.fold_in(streams_of[8], 71), 0),
    }


courant = 0.5
grad_scale = 0.125


def next_cell(field, axis):
    rest = lax.slice_in_dim(field, 1, field.shape[axis], axis=axis)
    edge = jnp.zeros_like(lax.slice_in_dim(field, 0, 1, axis=axis))
    return jnp.concatenate([rest, edge], axis=axis)


def prior_cell(field, axis):
    rest = lax.slice_in_dim(field, 0, field.shape[axis] - 1, axis=axis)
    edge = jnp.zeros_like(lax.slice_in_dim(field, 0, 1, axis=axis))
    return jnp.concatenate([edge, rest], axis=axis)


def material_coefficient(material, inv_eps):
    coefficient = jnp.zeros(material.shape, jnp.float32)
    for which in range(inv_eps.shape[0]):
        coefficient = coefficient + jnp.where(material == which, inv_eps[which], jnp.zeros((), jnp.float32))
    return courant * coefficient


def reference(adjoint_e, adjoint_h, material, inv_eps, forward_design, cell_slot, tile_pillars, pillar_rank):
    efield_x = adjoint_e[0].astype(jnp.float32)
    efield_y = adjoint_e[1].astype(jnp.float32)
    efield_z = adjoint_e[2].astype(jnp.float32)
    hnew_x = adjoint_h[0].astype(jnp.float32) - courant * ((next_cell(efield_z, 1) - efield_z) - (next_cell(efield_y, 2) - efield_y))
    hnew_y = adjoint_h[1].astype(jnp.float32) - courant * ((next_cell(efield_x, 2) - efield_x) - (next_cell(efield_z, 0) - efield_z))
    hnew_z = adjoint_h[2].astype(jnp.float32) - courant * ((next_cell(efield_y, 0) - efield_y) - (next_cell(efield_x, 1) - efield_x))
    new_h = lax.optimization_barrier(jnp.stack([hnew_x, hnew_y, hnew_z]).astype(jnp.bfloat16))
    magnetic_x = new_h[0].astype(jnp.float32)
    magnetic_y = new_h[1].astype(jnp.float32)
    magnetic_z = new_h[2].astype(jnp.float32)
    coefficient = material_coefficient(material, inv_eps)
    enew_x = efield_x + coefficient * ((magnetic_z - prior_cell(magnetic_z, 1)) - (magnetic_y - prior_cell(magnetic_y, 2)))
    enew_y = efield_y + coefficient * ((magnetic_x - prior_cell(magnetic_x, 2)) - (magnetic_z - prior_cell(magnetic_z, 0)))
    enew_z = efield_z + coefficient * ((magnetic_y - prior_cell(magnetic_y, 0)) - (magnetic_x - prior_cell(magnetic_x, 1)))
    new_e = jnp.stack([enew_x, enew_y, enew_z]).astype(jnp.bfloat16)
    offset = (NZ - DZ) // 2
    slab = lax.slice_in_dim(adjoint_e, offset, offset + DZ, axis=3).astype(jnp.float32)
    intersection_density = jnp.sum(slab * forward_design.astype(jnp.float32), axis=0)
    layer_sums = intersection_density.reshape(NX, NY, DL, DZ // DL).sum(axis=3)
    tile_x = (jnp.arange(NX) // CX).astype(jnp.int32)
    tile_y = (jnp.arange(NY) // CY).astype(jnp.int32)
    pillar_of = tile_pillars[tile_x[:, None], tile_y[None, :], cell_slot]
    pillar_sums = jax.ops.segment_sum(layer_sums.reshape(NX * NY, DL), pillar_of.reshape(-1), num_segments=P_SIZE)
    gradient = jnp.zeros((DL, P_SIZE), jnp.float32).at[:, pillar_rank].set(grad_scale * pillar_sums.T)
    return new_e, new_h, gradient
```

```python
import functools

import jax
import jax.numpy as jnp
from jax import lax
from jax.experimental import pallas as pl
from jax.experimental.pallas import tpu as pltpu
from jax.sharding import PartitionSpec as P

DL = 32

courant = 0.5
grad_scale = 0.125

MESH = pl.DeviceIdType.MESH
f32 = jnp.float32
bf16 = jnp.bfloat16
LANES = 128
BLOCK = 8


def iota(shape, axis):
    return lax.broadcasted_iota(jnp.int32, shape, axis)


def dot(a, b):
    return jnp.dot(a, b, preferred_element_type=f32)


def one_hot(mask):
    return jnp.where(mask, 1.0, 0.0).astype(bf16)


def split(value):
    high = value.astype(bf16)
    return high, (value - high.astype(f32)).astype(bf16)


def kernel(
    count_x,
    count_y,
    e_hbm,
    h_hbm,
    m_hbm,
    eps,
    f_hbm,
    cs_hbm,
    tp_hbm,
    pr_hbm,
    ne,
    nh,
    grad,
    e_v,
    h_v,
    m_v,
    f_v,
    cs_v,
    tp_v,
    pr_v,
    rt_v,
    acc,
    stage,
    out_y_prev,
    out_y_next,
    in_xn,
    in_xpe,
    in_xph,
    in_yn,
    in_yp,
    in_c1,
    in_c2,
    yn,
    hy_edge,
    send,
    recv,
    load_sem,
    face_send,
    face_recv,
    part_send,
    part_recv,
):
    _, cx, cy, nz = e_hbm.shape
    slots = tp_hbm.shape[2]
    devices = count_x * count_y
    half_x, half_y = cx // 2, cy // 2
    width = count_y * half_y
    rank_rows = pr_v.shape[0]
    per_device = slots // devices
    groups = LANES // DL
    rows = per_device // groups
    owned = pr_hbm.shape[0] * LANES // devices

    gx, gy = lax.axis_index("gx"), lax.axis_index("gy")
    me = gx * count_y + gy

    loads = [
        pltpu.make_async_copy(src, dst, load_sem.at[i])
        for i, (src, dst) in enumerate(
            [
                (e_hbm, e_v.at[:, pl.ds(0, cx)]),
                (h_hbm, h_v),
                (tp_hbm.at[gx], tp_v),
                (pr_hbm.at[pl.ds(pl.multiple_of(gx * rank_rows, 8), rank_rows)], pr_v),
                (cs_hbm, cs_v),
                (f_hbm, f_v),
                (m_hbm, m_v),
            ]
        )
    ]
    for load in loads:
        load.start()

    barrier = pltpu.get_barrier_semaphore()

    def partner(step):
        device = lax.rem(me + step, devices)
        return device, (lax.div(device, count_y), lax.rem(device, count_y))

    def greet(step, carry):
        pl.semaphore_signal(barrier, inc=1, device_id=partner(step)[1], device_id_type=MESH)
        return carry

    lax.fori_loop(1, devices, greet, 0)

    loads[0].wait()
    loads[1].wait()

    def gather_rows(x, carry):
        for c in range(3):
            first = e_v[c, x, 0:16, :].astype(f32)
            last = e_v[c, x, cy - 16 : cy, :].astype(f32)
            stage[c, pl.ds(x, 1), :] = first[0:1]
            stage[3 + c, pl.ds(x, 1), :] = last[15:16]
        for k, c in enumerate((0, 2)):
            stage[6 + k, pl.ds(x, 1), :] = h_v[c, x, cy - 16 : cy, :].astype(f32)[15:16]
        return carry

    lax.fori_loop(0, cx, gather_rows, 0)
    out_y_prev[0] = stage[0].astype(bf16)
    out_y_prev[1] = stage[2].astype(bf16)
    for k in range(5):
        out_y_next[k] = stage[3 + k].astype(bf16)

    pl.semaphore_wait(barrier, devices - 1)

    faces = [
        (e_hbm.at[pl.ds(1, 2), 0], in_xn, -1, 0),
        (out_y_prev, in_yn, 0, -1),
        (e_hbm.at[:, cx - 1], in_xpe, 1, 0),
        (h_hbm.at[pl.ds(1, 2), cx - 1], in_xph, 1, 0),
        (out_y_next, in_yp, 0, 1),
        (e_hbm.at[0, cx - 1, pl.ds(0, 16)], in_c1, 1, -1),
        (e_hbm.at[1, 0, pl.ds(cy - 16, 16)], in_c2, -1, 1),
    ]

    def inside(step_x, step_y):
        there = None
        for at, step, count in ((gx, step_x, count_x), (gy, step_y, count_y)):
            if step:
                fits = at + step < count if step > 0 else at + step >= 0
                there = fits if there is None else jnp.logical_and(there, fits)
        return there

    def face_copy(i):
        source, landing, step_x, step_y = faces[i]
        return pltpu.make_async_remote_copy(
            src_ref=source,
            dst_ref=landing,
            send_sem=face_send.at[i],
            recv_sem=face_recv.at[i],
            device_id=(gx + step_x, gy + step_y),
            device_id_type=MESH,
        )

    for i, (_, landing, step_x, step_y) in enumerate(faces):

        @pl.when(inside(step_x, step_y))
        def _():
            face_copy(i).start()

        @pl.when(jnp.logical_not(inside(-step_x, -step_y)))
        def _():
            landing[...] = jnp.zeros(landing.shape, landing.dtype)

    loads[2].wait()
    loads[3].wait()
    tile_row = iota(tp_v.shape, 0) == gy
    ids = jnp.sum(jnp.where(tile_row, tp_v[...], 0), axis=0, keepdims=True)
    listed = ids >= 0
    local = jnp.where(listed, ids - gx * (half_x * width), 0)
    local_row, local_lane = lax.div(local, LANES), lax.rem(local, LANES)
    ranks = pr_v[...]
    if rank_rows < LANES:
        ranks = jnp.concatenate(
            [ranks, jnp.zeros((LANES - rank_rows, LANES), jnp.int32)], axis=0
        )
    turned_high = lax.shift_right_logical(ranks, 8).astype(f32).T
    turned_low = lax.bitwise_and(ranks, 255).astype(f32).T
    table = jnp.concatenate([turned_high.astype(bf16), turned_low.astype(bf16)], axis=0)
    picked = dot(table, one_hot(iota((LANES, slots), 0) == local_row))
    picked = 256.0 * picked[:LANES] + picked[LANES:]
    slot_rank = jnp.sum(
        jnp.where(iota((LANES, slots), 0) == local_lane, picked, 0.0), axis=0, keepdims=True
    )
    turned = 256.0 * turned_high + turned_low
    along_y = lax.rem(iota((LANES, LANES), 1) * LANES + iota((LANES, LANES), 0), width)
    rt_v[...] = jnp.where(lax.div(along_y, half_y) == gy, turned, 1e9)
    tile_ranks = rt_v[
        pl.ds(pl.multiple_of(lax.rem(gy * half_y, LANES), half_y), half_y), :
    ]
    below = jnp.zeros((half_y, slots), f32)
    for j in range(rank_rows):
        below = below + jnp.where(tile_ranks[:, j : j + 1] < slot_rank, 1.0, 0.0)
    place = jnp.sum(below, axis=0, keepdims=True).astype(jnp.int32)
    owner, nth = lax.div(place, per_device), lax.rem(place, per_device)
    line = lax.div(nth, rows) * LANES + lax.rem(nth, rows) * devices + owner
    line = jnp.where(listed, line, -1)
    chosen = iota((slots, slots), 0) == line
    order = one_hot(chosen)
    own_rank = lax.rem(slot_rank.astype(jnp.int32), owned).astype(f32)
    rank_lines = jnp.sum(jnp.where(chosen, own_rank, 0.0), axis=1, keepdims=True)
    lane_group = lax.div(iota((LANES, LANES), 1), DL)
    rank_block = jnp.zeros((LANES, LANES), f32)
    for j in range(groups):
        rank_block = jnp.where(
            lane_group == j, rank_lines[j * LANES : (j + 1) * LANES], rank_block
        )

    loads[4].wait()
    loads[5].wait()
    batch = 256 // cy

    def add_cells(g, carry):
        slot_parts, parts = [], []
        for a in range(batch):
            x = g * batch + a
            slot_parts.append(cs_v[pl.ds(x, 1), :])
            density = e_v[0, x].astype(f32) * f_v[0, x].astype(f32)
            for c in (1, 2):
                density = density + e_v[c, x].astype(f32) * f_v[c, x].astype(f32)
            parts.append(jnp.concatenate(split(density), axis=1))
        cell_slots = jnp.concatenate(slot_parts, axis=1)
        hot = one_hot(iota((slots, batch * cy), 0) == cell_slots)
        acc[...] += dot(hot, jnp.concatenate(parts, axis=0))
        return carry

    acc[...] = jnp.zeros_like(acc)
    lax.fori_loop(0, cx // batch, add_cells, 0)
    sums = acc[:, :nz] + acc[:, nz:]
    sorted_sums = dot(order, jnp.concatenate(split(sums), axis=1)).astype(bf16)
    packed = jnp.concatenate(
        [
            jnp.concatenate(
                [
                    sorted_sums[j * LANES : (j + 1) * LANES, half * nz : (half + 1) * nz]
                    for j in range(groups)
                ],
                axis=1,
            )
            for half in range(2)
        ],
        axis=0,
    )
    pool_row, pool_lane = iota((groups * nz, LANES), 0), iota((groups * nz, LANES), 1)
    pool_to = lax.div(pool_row, nz) * DL + lax.div(lax.rem(pool_row, nz), nz // DL)
    pooled = dot(packed, one_hot(pool_to == pool_lane))
    pooled = pooled[:LANES] + pooled[LANES:]
    if 2 * rows < BLOCK:
        send[...] = jnp.zeros_like(send)
    for i in range(rows):
        part = slice(i * devices, (i + 1) * devices)
        send[pl.ds(i, devices, stride=BLOCK), :] = pooled[part]
        send[pl.ds(rows + i, devices, stride=BLOCK), :] = rank_block[part]

    mine = pl.ds(pl.multiple_of(me * BLOCK, BLOCK), BLOCK)

    def send_part(step, carry):
        device, where = partner(step)
        pltpu.make_async_remote_copy(
            src_ref=send.at[pl.ds(pl.multiple_of(device * BLOCK, BLOCK), BLOCK)],
            dst_ref=recv.at[mine],
            send_sem=part_send,
            recv_sem=part_recv,
            device_id=where,
            device_id_type=MESH,
        ).start()
        return carry

    lax.fori_loop(1, devices, send_part, 0)
    recv[mine, :] = send[mine, :]

    for i, (_, _, step_x, step_y) in enumerate(faces):

        @pl.when(inside(-step_x, -step_y))
        def _():
            face_copy(i).wait_recv()

    for c in (1, 2):
        e_v[c, cx] = in_xn[c - 1]
    for k in range(2):
        yn[k] = in_yn[k].astype(f32)

    last_lane = iota((1, nz), 1) == nz - 1
    first_lane = iota((1, nz), 1) == 0

    def next_z(field):
        return jnp.where(last_lane, 0.0, pltpu.roll(field, nz - 1, 1))

    def prior_z(field):
        return jnp.where(first_lane, 0.0, pltpu.roll(field, 1, 1))

    def next_row(field, edge):
        size = field.shape[0]
        return jnp.where(
            iota((size, 1), 0) == size - 1, edge, pltpu.roll(field, size - 1, 0)
        )

    def prior_row(field, edge):
        return jnp.where(iota((field.shape[0], 1), 0) == 0, edge, pltpu.roll(field, 1, 0))

    pe_x, pe_y, pe_z, ph_x, ph_z = [in_yp[k].astype(f32) for k in range(5)]
    first_x, first_z = stage[0], stage[2]
    edge_x = ph_x - courant * ((first_z - pe_z) - (next_z(pe_y) - pe_y))
    corner = in_c2[...].astype(f32)[15:16]
    edge_z = ph_z - courant * ((next_row(pe_y, corner) - pe_y) - (first_x - pe_x))
    keep_y = gy > 0
    hy_edge[0] = jnp.where(keep_y, edge_x, 0.0).astype(bf16).astype(f32)
    hy_edge[1] = jnp.where(keep_y, edge_z, 0.0).astype(bf16).astype(f32)

    pe_x, pe_y, pe_z = [in_xpe[k].astype(f32) for k in range(3)]
    ph_y, ph_z = [in_xph[k].astype(f32) for k in range(2)]
    first_y, first_z = e_v[1, 0].astype(f32), e_v[2, 0].astype(f32)
    back_y = ph_y - courant * ((next_z(pe_x) - pe_x) - (first_z - pe_z))
    corner = in_c1[...].astype(f32)[0:1]
    back_z = ph_z - courant * ((first_y - pe_y) - (next_row(pe_x, corner) - pe_x))
    keep_x = gx > 0
    back_y = jnp.where(keep_x, back_y, 0.0).astype(bf16)
    back_z = jnp.where(keep_x, back_z, 0.0).astype(bf16)

    loads[6].wait()
    factors = [courant * eps[k] for k in range(eps.shape[0])]

    def update(x, carry):
        back_y, back_z = [value.astype(f32) for value in carry]
        e_x, e_y, e_z = [e_v[c, x].astype(f32) for c in range(3)]
        nx_y, nx_z = [e_v[c, x + 1].astype(f32) for c in (1, 2)]
        ny_x, ny_z = [yn[k, pl.ds(x, 1), :] for k in range(2)]
        d_y_z, d_z_y = next_row(e_z, ny_z) - e_z, next_z(e_y) - e_y
        h_x = (h_v[0, x].astype(f32) - courant * (d_y_z - d_z_y)).astype(bf16)
        d_z_x, d_x_z = next_z(e_x) - e_x, nx_z - e_z
        h_y = (h_v[1, x].astype(f32) - courant * (d_z_x - d_x_z)).astype(bf16)
        d_x_y, d_y_x = nx_y - e_y, next_row(e_x, ny_x) - e_x
        h_z = (h_v[2, x].astype(f32) - courant * (d_x_y - d_y_x)).astype(bf16)
        nh[0, x], nh[1, x], nh[2, x] = h_x, h_y, h_z
        ahead = (h_y, h_z)
        h_x, h_y, h_z = h_x.astype(f32), h_y.astype(f32), h_z.astype(f32)
        before_x, before_z = [hy_edge[k, pl.ds(x, 1), :] for k in range(2)]
        material = m_v[x]
        factor = jnp.full(material.shape, factors[-1], f32)
        for which in range(len(factors) - 1):
            factor = jnp.where(material == which, factors[which], factor)
        b_y_z, b_z_y = h_z - prior_row(h_z, before_z), h_y - prior_z(h_y)
        ne[0, x] = (e_x + factor * (b_y_z - b_z_y)).astype(bf16)
        b_z_x, b_x_z = h_x - prior_z(h_x), h_z - back_z
        ne[1, x] = (e_y + factor * (b_z_x - b_x_z)).astype(bf16)
        b_x_y, b_y_x = h_y - back_y, h_x - prior_row(h_x, before_x)
        ne[2, x] = (e_z + factor * (b_x_y - b_y_x)).astype(bf16)
        return ahead

    lax.fori_loop(0, cx, update, (back_y, back_z))

    others = pl.ds(0, (devices - 1) * BLOCK)
    arrivals = pltpu.make_async_remote_copy(
        src_ref=send.at[others],
        dst_ref=recv.at[others],
        send_sem=part_send,
        recv_sem=part_recv,
        device_id=(gx, gy),
        device_id_type=MESH,
    )
    arrivals.wait_recv()
    values = jnp.concatenate(
        [recv[pl.ds(i, devices, stride=BLOCK), :] for i in range(rows)], axis=0
    )
    value_ranks = jnp.concatenate(
        [recv[pl.ds(rows + i, devices, stride=BLOCK), :] for i in range(rows)], axis=0
    )
    turned_values = values.T
    terms = jnp.concatenate(
        [turned_values[j * DL : (j + 1) * DL] for j in range(groups)], axis=1
    )
    lane_rank = iota((LANES, owned), 1).astype(f32)
    target = jnp.concatenate(
        [one_hot(value_ranks[:, j * DL : j * DL + 1] == lane_rank) for j in range(groups)],
        axis=0,
    )
    result = dot(jnp.concatenate(split(terms), axis=0), target)
    grad[...] = grad_scale * (result[:DL] + result[DL:])

    arrivals.wait_send()
    for i, (_, _, step_x, step_y) in enumerate(faces):

        @pl.when(inside(step_x, step_y))
        def _():
            face_copy(i).wait_send()


def per_device(
    adjoint_e, adjoint_h, material, inv_eps, forward_design, cell_slot, tile_pillars, pillar_rank
):
    count_x, count_y = lax.axis_size("gx"), lax.axis_size("gy")
    devices = count_x * count_y
    _, cx, cy, nz = adjoint_e.shape
    slots = tile_pillars.shape[2]
    ranks = pillar_rank.reshape(-1, LANES)
    rank_rows = ranks.shape[0] // count_x
    owned = pillar_rank.shape[0] // devices
    anywhere = pl.BlockSpec(memory_space=pl.ANY)
    vmem = pl.BlockSpec(memory_space=pltpu.VMEM)
    return pl.pallas_call(
        functools.partial(kernel, count_x, count_y),
        out_shape=(
            jax.ShapeDtypeStruct(adjoint_e.shape, bf16),
            jax.ShapeDtypeStruct(adjoint_h.shape, bf16),
            jax.ShapeDtypeStruct((DL, owned), f32),
        ),
        in_specs=[
            anywhere,
            anywhere,
            anywhere,
            pl.BlockSpec(memory_space=pltpu.SMEM),
            anywhere,
            anywhere,
            anywhere,
            anywhere,
        ],
        out_specs=(vmem, vmem, vmem),
        scratch_shapes=[
            pltpu.VMEM((3, cx + 1, cy, nz), bf16),
            pltpu.VMEM((3, cx, cy, nz), bf16),
            pltpu.VMEM((cx, cy, nz), jnp.int32),
            pltpu.VMEM((3, cx, cy, nz), bf16),
            pltpu.VMEM((cx, cy), jnp.int32),
            pltpu.VMEM((count_y, slots), jnp.int32),
            pltpu.VMEM((rank_rows, LANES), jnp.int32),
            pltpu.VMEM((LANES, LANES), f32),
            pltpu.VMEM((slots, 2 * nz), f32),
            pltpu.VMEM((8, cx, nz), f32),
            pltpu.VMEM((2, cx, nz), bf16),
            pltpu.VMEM((5, cx, nz), bf16),
            pltpu.VMEM((2, cy, nz), bf16),
            pltpu.VMEM((3, cy, nz), bf16),
            pltpu.VMEM((2, cy, nz), bf16),
            pltpu.VMEM((2, cx, nz), bf16),
            pltpu.VMEM((5, cx, nz), bf16),
            pltpu.VMEM((16, nz), bf16),
            pltpu.VMEM((16, nz), bf16),
            pltpu.VMEM((2, cx, nz), f32),
            pltpu.VMEM((2, cx, nz), f32),
            pltpu.VMEM((devices * BLOCK, LANES), f32),
            pltpu.VMEM((devices * BLOCK, LANES), f32),
            pltpu.SemaphoreType.DMA((7,)),
            pltpu.SemaphoreType.DMA((7,)),
            pltpu.SemaphoreType.DMA((7,)),
            pltpu.SemaphoreType.DMA,
            pltpu.SemaphoreType.DMA,
        ],
        compiler_params=pltpu.CompilerParams(
            collective_id=0, has_side_effects=True, vmem_limit_bytes=48 * 1024 * 1024
        ),
    )(
        adjoint_e,
        adjoint_h,
        material,
        inv_eps,
        forward_design,
        cell_slot,
        tile_pillars,
        ranks,
    )


def solution(mesh):
    return jax.shard_map(
        per_device,
        mesh=mesh,
        in_specs=(
            P(None, "gx", "gy", None),
            P(None, "gx", "gy", None),
            P("gx", "gy", None),
            P(),
            P(None, "gx", "gy", None),
            P("gx", "gy"),
            P(),
            P(),
        ),
        out_specs=(P(None, "gx", "gy", None), P(None, "gx", "gy", None), P(None, ("gx", "gy"))),
        check_vma=False,
    )
```

```python
import functools

import jax
import jax.numpy as jnp
from jax import lax
from jax.experimental import pallas as pl
from jax.experimental.pallas import tpu as pltpu
from jax.sharding import PartitionSpec as P

DL = 32

courant = 0.5
grad_scale = 0.125

MESH = pl.DeviceIdType.MESH
f32 = jnp.float32
bf16 = jnp.bfloat16
LANES = 128
BLOCK = 8


def iota(shape, axis):
    return lax.broadcasted_iota(jnp.int32, shape, axis)


def dot(a, b):
    return jnp.dot(a, b, preferred_element_type=f32)


def one_hot(mask):
    return jnp.where(mask, 1.0, 0.0).astype(bf16)


def split(value):
    high = value.astype(bf16)
    return high, (value - high.astype(f32)).astype(bf16)


def next_z(field):
    size = field.shape[1]
    return jnp.where(iota((1, size), 1) == size - 1, 0.0, pltpu.roll(field, size - 1, 1))


def prior_z(field):
    return jnp.where(iota((1, field.shape[1]), 1) == 0, 0.0, pltpu.roll(field, 1, 1))


def next_row(field, edge):
    size = field.shape[0]
    return jnp.where(iota((size, 1), 0) == size - 1, edge, pltpu.roll(field, size - 1, 0))


def prior_row(field, edge):
    return jnp.where(iota((field.shape[0], 1), 0) == 0, edge, pltpu.roll(field, 1, 0))


def exchange(
    count_x,
    count_y,
    e_hbm,
    h_hbm,
    m_hbm,
    eps_hbm,
    f_hbm,
    cs_hbm,
    tp_hbm,
    pr_hbm,
    e_v,
    nh,
    m_v,
    factors,
    hx_edge,
    hy_edge,
    recv,
    h_v,
    f_v,
    eps_v,
    cs_v,
    tp_v,
    pr_v,
    rt_v,
    acc,
    stage,
    out_y_prev,
    out_y_next,
    in_xn,
    in_xpe,
    in_xph,
    in_yn,
    in_yp,
    in_c1,
    in_c2,
    yn,
    send,
    load_sem,
    face_send,
    face_recv,
    part_send,
    part_recv,
):
    _, cx, cy, nz = e_hbm.shape
    slots = tp_hbm.shape[2]
    devices = count_x * count_y
    half_x, half_y = cx // 2, cy // 2
    width = count_y * half_y
    rank_rows = pr_v.shape[0]
    per_device = slots // devices
    groups = LANES // DL
    rows = per_device // groups
    owned = pr_hbm.shape[0] * LANES // devices

    gx, gy = lax.axis_index("gx"), lax.axis_index("gy")
    me = gx * count_y + gy

    loads = [
        pltpu.make_async_copy(src, dst, load_sem.at[i])
        for i, (src, dst) in enumerate(
            [
                (tp_hbm.at[gx], tp_v),
                (pr_hbm.at[pl.ds(pl.multiple_of(gx * rank_rows, 8), rank_rows)], pr_v),
                (e_hbm, e_v.at[:, pl.ds(0, cx)]),
                (h_hbm, h_v),
                (cs_hbm, cs_v),
                (f_hbm, f_v),
                (eps_hbm, eps_v),
                (m_hbm, m_v),
            ]
        )
    ]
    for load in loads:
        load.start()

    barrier = pltpu.get_barrier_semaphore()

    def partner(step):
        device = lax.rem(me + step, devices)
        return device, (lax.div(device, count_y), lax.rem(device, count_y))

    def greet(step, carry):
        pl.semaphore_signal(barrier, inc=1, device_id=partner(step)[1], device_id_type=MESH)
        return carry

    lax.fori_loop(1, devices, greet, 0)

    loads[0].wait()
    loads[1].wait()
    tile_row = iota(tp_v.shape, 0) == gy
    ids = jnp.sum(jnp.where(tile_row, tp_v[...], 0), axis=0, keepdims=True)
    listed = ids >= 0
    local = jnp.where(listed, ids - gx * (half_x * width), 0)
    local_row, local_lane = lax.div(local, LANES), lax.rem(local, LANES)
    ranks = pr_v[...]
    if rank_rows < LANES:
        ranks = jnp.concatenate(
            [ranks, jnp.zeros((LANES - rank_rows, LANES), jnp.int32)], axis=0
        )
    turned_high = lax.shift_right_logical(ranks, 8).astype(f32).T
    turned_low = lax.bitwise_and(ranks, 255).astype(f32).T
    table = jnp.concatenate([turned_high.astype(bf16), turned_low.astype(bf16)], axis=0)
    picked = dot(table, one_hot(iota((LANES, slots), 0) == local_row))
    picked = 256.0 * picked[:LANES] + picked[LANES:]
    slot_rank = jnp.sum(
        jnp.where(iota((LANES, slots), 0) == local_lane, picked, 0.0), axis=0, keepdims=True
    )
    turned = 256.0 * turned_high + turned_low
    along_y = lax.rem(iota((LANES, LANES), 1) * LANES + iota((LANES, LANES), 0), width)
    rt_v[...] = jnp.where(lax.div(along_y, half_y) == gy, turned, 1e9)
    tile_ranks = rt_v[
        pl.ds(pl.multiple_of(lax.rem(gy * half_y, LANES), half_y), half_y), :
    ]
    below = jnp.zeros((half_y, slots), f32)
    for j in range(rank_rows):
        below = below + jnp.where(tile_ranks[:, j : j + 1] < slot_rank, 1.0, 0.0)
    place = jnp.sum(below, axis=0, keepdims=True).astype(jnp.int32)
    owner, nth = lax.div(place, per_device), lax.rem(place, per_device)
    line = lax.div(nth, rows) * LANES + lax.rem(nth, rows) * devices + owner
    line = jnp.where(listed, line, -1)
    chosen = iota((slots, slots), 0) == line
    order = one_hot(chosen)
    own_rank = lax.rem(slot_rank.astype(jnp.int32), owned).astype(f32)
    rank_lines = jnp.sum(jnp.where(chosen, own_rank, 0.0), axis=1, keepdims=True)
    lane_group = lax.div(iota((LANES, LANES), 1), DL)
    rank_block = jnp.zeros((LANES, LANES), f32)
    for j in range(groups):
        rank_block = jnp.where(
            lane_group == j, rank_lines[j * LANES : (j + 1) * LANES], rank_block
        )

    loads[2].wait()
    loads[3].wait()

    def gather_rows(x, carry):
        for c in range(3):
            first = e_v[c, x, 0:16, :].astype(f32)
            last = e_v[c, x, cy - 16 : cy, :].astype(f32)
            stage[c, pl.ds(x, 1), :] = first[0:1]
            stage[3 + c, pl.ds(x, 1), :] = last[15:16]
        for k, c in enumerate((0, 2)):
            stage[6 + k, pl.ds(x, 1), :] = h_v[c, x, cy - 16 : cy, :].astype(f32)[15:16]
        return carry

    lax.fori_loop(0, cx, gather_rows, 0, unroll=4)
    out_y_prev[0] = stage[0].astype(bf16)
    out_y_prev[1] = stage[2].astype(bf16)
    for k in range(5):
        out_y_next[k] = stage[3 + k].astype(bf16)

    pl.semaphore_wait(barrier, devices - 1)

    faces = [
        (e_hbm.at[pl.ds(1, 2), 0], in_xn, -1, 0),
        (out_y_prev, in_yn, 0, -1),
        (e_hbm.at[:, cx - 1], in_xpe, 1, 0),
        (h_hbm.at[pl.ds(1, 2), cx - 1], in_xph, 1, 0),
        (out_y_next, in_yp, 0, 1),
        (e_hbm.at[0, cx - 1, pl.ds(0, 16)], in_c1, 1, -1),
        (e_hbm.at[1, 0, pl.ds(cy - 16, 16)], in_c2, -1, 1),
    ]

    def inside(step_x, step_y):
        there = None
        for at, step, count in ((gx, step_x, count_x), (gy, step_y, count_y)):
            if step:
                fits = at + step < count if step > 0 else at + step >= 0
                there = fits if there is None else jnp.logical_and(there, fits)
        return there

    def face_copy(i):
        source, landing, step_x, step_y = faces[i]
        return pltpu.make_async_remote_copy(
            src_ref=source,
            dst_ref=landing,
            send_sem=face_send.at[i],
            recv_sem=face_recv.at[i],
            device_id=(gx + step_x, gy + step_y),
            device_id_type=MESH,
        )

    for i, (_, landing, step_x, step_y) in enumerate(faces):

        @pl.when(inside(step_x, step_y))
        def _():
            face_copy(i).start()

        @pl.when(jnp.logical_not(inside(-step_x, -step_y)))
        def _():
            landing[...] = jnp.zeros(landing.shape, landing.dtype)

    loads[4].wait()
    loads[5].wait()
    batch = 256 // cy

    def add_cells(g, carry):
        slot_parts, parts = [], []
        for a in range(batch):
            x = g * batch + a
            slot_parts.append(cs_v[pl.ds(x, 1), :])
            density = e_v[0, x].astype(f32) * f_v[0, x].astype(f32)
            for c in (1, 2):
                density = density + e_v[c, x].astype(f32) * f_v[c, x].astype(f32)
            parts.append(jnp.concatenate(split(density), axis=1))
        cell_slots = jnp.concatenate(slot_parts, axis=1)
        hot = one_hot(iota((slots, batch * cy), 0) == cell_slots)
        acc[...] += dot(hot, jnp.concatenate(parts, axis=0))
        return carry

    acc[...] = jnp.zeros_like(acc)
    lax.fori_loop(0, cx // batch, add_cells, 0, unroll=2)
    sums = acc[:, :nz] + acc[:, nz:]
    sorted_sums = dot(order, jnp.concatenate(split(sums), axis=1)).astype(bf16)
    packed = jnp.concatenate(
        [
            jnp.concatenate(
                [
                    sorted_sums[j * LANES : (j + 1) * LANES, half * nz : (half + 1) * nz]
                    for j in range(groups)
                ],
                axis=1,
            )
            for half in range(2)
        ],
        axis=0,
    )
    layer = lax.div(iota((nz, LANES), 0), nz // DL)
    lane = iota((nz, LANES), 1)
    pool = jnp.concatenate([one_hot(layer + j * DL == lane) for j in range(groups)], axis=0)
    pooled = dot(packed, pool)
    pooled = pooled[:LANES] + pooled[LANES:]
    if 2 * rows < BLOCK:
        send[...] = jnp.zeros_like(send)
    for i in range(rows):
        part = slice(i * devices, (i + 1) * devices)
        send[pl.ds(i, devices, stride=BLOCK), :] = pooled[part]
        send[pl.ds(rows + i, devices, stride=BLOCK), :] = rank_block[part]

    mine = pl.ds(pl.multiple_of(me * BLOCK, BLOCK), BLOCK)

    def send_part(step, carry):
        device, where = partner(step)
        pltpu.make_async_remote_copy(
            src_ref=send.at[pl.ds(pl.multiple_of(device * BLOCK, BLOCK), BLOCK)],
            dst_ref=recv.at[mine],
            send_sem=part_send,
            recv_sem=part_recv,
            device_id=where,
            device_id_type=MESH,
        ).start()
        return carry

    lax.fori_loop(1, devices, send_part, 0)
    recv[mine, :] = send[mine, :]

    for i, (_, _, step_x, step_y) in enumerate(faces):

        @pl.when(inside(-step_x, -step_y))
        def _():
            face_copy(i).wait_recv()

    for c in (1, 2):
        e_v[c, cx] = in_xn[c - 1]
    for k in range(2):
        yn[k] = in_yn[k].astype(f32)

    pe_x, pe_y, pe_z, ph_x, ph_z = [in_yp[k].astype(f32) for k in range(5)]
    first_x, first_z = stage[0], stage[2]
    edge_x = ph_x - courant * ((first_z - pe_z) - (next_z(pe_y) - pe_y))
    corner = in_c2[...].astype(f32)[15:16]
    edge_z = ph_z - courant * ((next_row(pe_y, corner) - pe_y) - (first_x - pe_x))
    keep_y = gy > 0
    hy_edge[0] = jnp.where(keep_y, edge_x, 0.0).astype(bf16).astype(f32)
    hy_edge[1] = jnp.where(keep_y, edge_z, 0.0).astype(bf16).astype(f32)

    pe_x, pe_y, pe_z = [in_xpe[k].astype(f32) for k in range(3)]
    ph_y, ph_z = [in_xph[k].astype(f32) for k in range(2)]
    first_y, first_z = e_v[1, 0].astype(f32), e_v[2, 0].astype(f32)
    back_y = ph_y - courant * ((next_z(pe_x) - pe_x) - (first_z - pe_z))
    corner = in_c1[...].astype(f32)[0:1]
    back_z = ph_z - courant * ((first_y - pe_y) - (next_row(pe_x, corner) - pe_x))
    keep_x = gx > 0
    hx_edge[0] = jnp.where(keep_x, back_y, 0.0).astype(bf16)
    hx_edge[1] = jnp.where(keep_x, back_z, 0.0).astype(bf16)

    def update_h(x, carry):
        e_x, e_y, e_z = [e_v[c, x].astype(f32) for c in range(3)]
        nx_y, nx_z = [e_v[c, x + 1].astype(f32) for c in (1, 2)]
        ny_x, ny_z = [yn[k, pl.ds(x, 1), :] for k in range(2)]
        d_y_z, d_z_y = next_row(e_z, ny_z) - e_z, next_z(e_y) - e_y
        nh[0, x] = (h_v[0, x].astype(f32) - courant * (d_y_z - d_z_y)).astype(bf16)
        d_z_x, d_x_z = next_z(e_x) - e_x, nx_z - e_z
        nh[1, x] = (h_v[1, x].astype(f32) - courant * (d_z_x - d_x_z)).astype(bf16)
        d_x_y, d_y_x = nx_y - e_y, next_row(e_x, ny_x) - e_x
        nh[2, x] = (h_v[2, x].astype(f32) - courant * (d_x_y - d_y_x)).astype(bf16)
        return carry

    lax.fori_loop(0, cx, update_h, 0, unroll=4)

    loads[6].wait()
    for k in range(eps_v.shape[0]):
        factors[k : k + 1, :] = jnp.full((1, LANES), courant * eps_v[k], f32)
    loads[7].wait()

    others = pl.ds(0, (devices - 1) * BLOCK)
    arrivals = pltpu.make_async_remote_copy(
        src_ref=send.at[others],
        dst_ref=recv.at[others],
        send_sem=part_send,
        recv_sem=part_recv,
        device_id=(gx, gy),
        device_id_type=MESH,
    )
    arrivals.wait_recv()
    arrivals.wait_send()
    for i, (_, _, step_x, step_y) in enumerate(faces):

        @pl.when(inside(step_x, step_y))
        def _():
            face_copy(i).wait_send()


def finish(
    materials,
    e_v,
    nh_v,
    m_v,
    factors,
    hx_edge,
    hy_edge,
    recv,
    ne,
    nh,
    grad,
    ne_v,
    grad_v,
    store_sem,
):
    _, cx, cy, nz = nh_v.shape
    devices = recv.shape[0] // BLOCK
    owned = grad.shape[1]
    groups = LANES // DL
    rows = owned // devices // groups
    chunks = 4
    depth = cx // chunks

    stores = [
        pltpu.make_async_copy(nh_v, nh, store_sem.at[0]),
        pltpu.make_async_copy(grad_v, grad, store_sem.at[1]),
    ] + [
        pltpu.make_async_copy(
            ne_v.at[:, pl.ds(k * depth, depth)],
            ne.at[:, pl.ds(k * depth, depth)],
            store_sem.at[2 + k],
        )
        for k in range(chunks)
    ]
    stores[0].start()

    values = jnp.concatenate(
        [recv[pl.ds(i, devices, stride=BLOCK), :] for i in range(rows)], axis=0
    )
    value_ranks = jnp.concatenate(
        [recv[pl.ds(rows + i, devices, stride=BLOCK), :] for i in range(rows)], axis=0
    )
    turned_values = values.T
    terms = jnp.concatenate(
        [turned_values[j * DL : (j + 1) * DL] for j in range(groups)], axis=1
    )
    lane_rank = iota((LANES, owned), 1).astype(f32)
    target = jnp.concatenate(
        [one_hot(value_ranks[:, j * DL : j * DL + 1] == lane_rank) for j in range(groups)],
        axis=0,
    )
    result = dot(jnp.concatenate(split(terms), axis=0), target)
    grad_v[...] = grad_scale * (result[:DL] + result[DL:])

    stores[1].start()

    row_factors = [factors[k : k + 1, :] for k in range(materials)]

    def update_e(x, carry):
        back_y, back_z = [value.astype(f32) for value in carry]
        ahead = nh_v[1, x], nh_v[2, x]
        h_x = nh_v[0, x].astype(f32)
        h_y, h_z = [value.astype(f32) for value in ahead]
        before_x, before_z = [hy_edge[k, pl.ds(x, 1), :] for k in range(2)]
        material = m_v[x]
        factor = jnp.broadcast_to(row_factors[-1], material.shape)
        for which in range(materials - 1):
            factor = jnp.where(material == which, row_factors[which], factor)
        b_y_z, b_z_y = h_z - prior_row(h_z, before_z), h_y - prior_z(h_y)
        ne_v[0, x] = (e_v[0, x].astype(f32) + factor * (b_y_z - b_z_y)).astype(bf16)
        b_z_x, b_x_z = h_x - prior_z(h_x), h_z - back_z
        ne_v[1, x] = (e_v[1, x].astype(f32) + factor * (b_z_x - b_x_z)).astype(bf16)
        b_x_y, b_y_x = h_y - back_y, h_x - prior_row(h_x, before_x)
        ne_v[2, x] = (e_v[2, x].astype(f32) + factor * (b_x_y - b_y_x)).astype(bf16)
        return ahead

    carry = hx_edge[0], hx_edge[1]
    for k in range(chunks):
        carry = lax.fori_loop(k * depth, (k + 1) * depth, update_e, carry, unroll=4)
        stores[2 + k].start()
    for store in stores:
        store.wait()


def per_device(
    adjoint_e, adjoint_h, material, inv_eps, forward_design, cell_slot, tile_pillars, pillar_rank
):
    count_x, count_y = lax.axis_size("gx"), lax.axis_size("gy")
    devices = count_x * count_y
    _, cx, cy, nz = adjoint_e.shape
    slots = tile_pillars.shape[2]
    ranks = pillar_rank.reshape(-1, LANES)
    rank_rows = ranks.shape[0] // count_x
    owned = pillar_rank.shape[0] // devices
    anywhere = pl.BlockSpec(memory_space=pl.ANY)
    vmem = pl.BlockSpec(memory_space=pltpu.VMEM)
    operands = [
        pltpu.with_memory_space_constraint(operand, pltpu.HBM)
        for operand in (
            adjoint_e,
            adjoint_h,
            material,
            inv_eps,
            forward_design,
            cell_slot,
            tile_pillars,
            ranks,
        )
    ]
    kept = pl.pallas_call(
        functools.partial(exchange, count_x, count_y),
        out_shape=(
            pltpu.VMEM((3, cx + 1, cy, nz), bf16),
            pltpu.VMEM((3, cx, cy, nz), bf16),
            pltpu.VMEM((cx, cy, nz), jnp.int32),
            pltpu.VMEM((8, LANES), f32),
            pltpu.VMEM((2, cy, nz), bf16),
            pltpu.VMEM((2, cx, nz), f32),
            pltpu.VMEM((devices * BLOCK, LANES), f32),
        ),
        in_specs=[anywhere] * 8,
        out_specs=(vmem,) * 7,
        scratch_shapes=[
            pltpu.VMEM((3, cx, cy, nz), bf16),
            pltpu.VMEM((3, cx, cy, nz), bf16),
            pltpu.SMEM(inv_eps.shape, f32),
            pltpu.VMEM((cx, cy), jnp.int32),
            pltpu.VMEM((count_y, slots), jnp.int32),
            pltpu.VMEM((rank_rows, LANES), jnp.int32),
            pltpu.VMEM((LANES, LANES), f32),
            pltpu.VMEM((slots, 2 * nz), f32),
            pltpu.VMEM((8, cx, nz), f32),
            pltpu.VMEM((2, cx, nz), bf16),
            pltpu.VMEM((5, cx, nz), bf16),
            pltpu.VMEM((2, cy, nz), bf16),
            pltpu.VMEM((3, cy, nz), bf16),
            pltpu.VMEM((2, cy, nz), bf16),
            pltpu.VMEM((2, cx, nz), bf16),
            pltpu.VMEM((5, cx, nz), bf16),
            pltpu.VMEM((16, nz), bf16),
            pltpu.VMEM((16, nz), bf16),
            pltpu.VMEM((2, cx, nz), f32),
            pltpu.VMEM((devices * BLOCK, LANES), f32),
            pltpu.SemaphoreType.DMA((8,)),
            pltpu.SemaphoreType.DMA((7,)),
            pltpu.SemaphoreType.DMA((7,)),
            pltpu.SemaphoreType.DMA,
            pltpu.SemaphoreType.DMA,
        ],
        compiler_params=pltpu.CompilerParams(
            collective_id=0, has_side_effects=True, vmem_limit_bytes=24 * 1024 * 1024
        ),
    )(*operands)
    return pl.pallas_call(
        functools.partial(finish, inv_eps.shape[0]),
        out_shape=(
            pltpu.HBM(adjoint_e.shape, bf16),
            pltpu.HBM(adjoint_h.shape, bf16),
            pltpu.HBM((DL, owned), f32),
        ),
        in_specs=[vmem] * 7,
        out_specs=(anywhere,) * 3,
        scratch_shapes=[
            pltpu.VMEM((3, cx, cy, nz), bf16),
            pltpu.VMEM((DL, owned), f32),
            pltpu.SemaphoreType.DMA((6,)),
        ],
        compiler_params=pltpu.CompilerParams(vmem_limit_bytes=16 * 1024 * 1024),
    )(*[pltpu.with_memory_space_constraint(value, pltpu.VMEM) for value in kept])


def solution(mesh):
    return jax.shard_map(
        per_device,
        mesh=mesh,
        in_specs=(
            P(None, "gx", "gy", None),
            P(None, "gx", "gy", None),
            P("gx", "gy", None),
            P(),
            P(None, "gx", "gy", None),
            P("gx", "gy"),
            P(),
            P(),
        ),
        out_specs=(P(None, "gx", "gy", None), P(None, "gx", "gy", None), P(None, ("gx", "gy"))),
        check_vma=False,
    )
```

```python
import functools

import jax
import jax.numpy as jnp
from jax import lax
from jax.experimental import pallas as pl
from jax.experimental.pallas import tpu as pltpu
from jax.sharding import PartitionSpec as P

DL = 32

courant = 0.5
grad_scale = 0.125

MESH = pl.DeviceIdType.MESH
f32 = jnp.float32
bf16 = jnp.bfloat16
LANES = 128
BLOCK = 8


def iota(shape, axis):
    return lax.broadcasted_iota(jnp.int32, shape, axis)


def dot(a, b):
    return jnp.dot(a, b, preferred_element_type=f32)


def one_hot(mask):
    return jnp.where(mask, 1.0, 0.0).astype(bf16)


def hot_rows(count, row):
    size = row.shape[1]
    number = iota((count, size), 0).astype(jnp.int16).reshape(count // 16, 16, size)
    entry = jnp.broadcast_to(row, (16, size)).astype(jnp.int16)
    hot = jnp.where(number == entry[None], jnp.ones((), bf16), jnp.zeros((), bf16))
    return hot.reshape(count, size)


def split(value):
    high = value.astype(bf16)
    return high, (value - high.astype(f32)).astype(bf16)


def next_z(field):
    size = field.shape[1]
    return jnp.where(iota((1, size), 1) == size - 1, 0.0, pltpu.roll(field, size - 1, 1))


def prior_z(field):
    return jnp.where(iota((1, field.shape[1]), 1) == 0, 0.0, pltpu.roll(field, 1, 1))


def next_row(field, edge):
    size = field.shape[0]
    return jnp.where(iota((size, 1), 0) == size - 1, edge, pltpu.roll(field, size - 1, 0))


def prior_row(field, edge):
    return jnp.where(iota((field.shape[0], 1), 0) == 0, edge, pltpu.roll(field, 1, 0))


def exchange(
    count_x,
    count_y,
    e_hbm,
    h_hbm,
    m_hbm,
    eps_hbm,
    f_hbm,
    cs_hbm,
    tp_hbm,
    pr_hbm,
    ne,
    nh,
    recv,
    e_v,
    m_v,
    hx_edge,
    hy_edge,
    h_v,
    f_v,
    eps_v,
    cs_v,
    tp_v,
    pr_v,
    rt_v,
    acc,
    stage,
    out_y_prev,
    out_y_next,
    in_xn,
    in_xpe,
    in_xph,
    in_yn,
    in_yp,
    in_c1,
    in_c2,
    yn,
    send,
    load_sem,
    face_send,
    face_recv,
    part_send,
    part_recv,
):
    _, cx, cy, nz = e_hbm.shape
    slots = tp_hbm.shape[2]
    devices = count_x * count_y
    half_x, half_y = cx // 2, cy // 2
    width = count_y * half_y
    rank_rows = pr_v.shape[0]
    per_device = slots // devices
    groups = LANES // DL
    rows = per_device // groups
    owned = pr_hbm.shape[0] * LANES // devices

    gx, gy = lax.axis_index("gx"), lax.axis_index("gy")
    me = gx * count_y + gy

    loads = [
        pltpu.make_async_copy(src, dst, load_sem.at[i])
        for i, (src, dst) in enumerate(
            [
                (tp_hbm.at[gx], tp_v),
                (pr_hbm.at[pl.ds(pl.multiple_of(gx * rank_rows, 8), rank_rows)], pr_v),
                (e_hbm, e_v.at[:, pl.ds(0, cx)]),
                (h_hbm, h_v),
                (cs_hbm, cs_v),
                (f_hbm, f_v),
                (eps_hbm, eps_v),
                (m_hbm, m_v),
            ]
        )
    ]
    for load in loads:
        load.start()

    barrier = pltpu.get_barrier_semaphore()

    def partner(step):
        device = lax.rem(me + step, devices)
        return device, (lax.div(device, count_y), lax.rem(device, count_y))

    def greet(step, carry):
        pl.semaphore_signal(barrier, inc=1, device_id=partner(step)[1], device_id_type=MESH)
        return carry

    lax.fori_loop(1, devices, greet, 0)

    loads[0].wait()
    loads[1].wait()
    tile_row = iota(tp_v.shape, 0) == gy
    ids = jnp.sum(jnp.where(tile_row, tp_v[...], 0), axis=0, keepdims=True)
    listed = ids >= 0
    local = jnp.where(listed, ids - gx * (half_x * width), 0)
    local_row, local_lane = lax.div(local, LANES), lax.rem(local, LANES)
    ranks = pr_v[...]
    if rank_rows < LANES:
        ranks = jnp.concatenate(
            [ranks, jnp.zeros((LANES - rank_rows, LANES), jnp.int32)], axis=0
        )
    turned_high = lax.shift_right_logical(ranks, 8).astype(f32).T
    turned_low = lax.bitwise_and(ranks, 255).astype(f32).T
    table = jnp.concatenate([turned_high.astype(bf16), turned_low.astype(bf16)], axis=0)
    picked = dot(table, one_hot(iota((LANES, slots), 0) == local_row))
    picked = 256.0 * picked[:LANES] + picked[LANES:]
    slot_rank = jnp.sum(
        jnp.where(iota((LANES, slots), 0) == local_lane, picked, 0.0), axis=0, keepdims=True
    )
    turned = 256.0 * turned_high + turned_low
    along_y = lax.rem(iota((LANES, LANES), 1) * LANES + iota((LANES, LANES), 0), width)
    rt_v[...] = jnp.where(lax.div(along_y, half_y) == gy, turned, 1e9)
    tile_ranks = rt_v[
        pl.ds(pl.multiple_of(lax.rem(gy * half_y, LANES), half_y), half_y), :
    ]
    below = jnp.zeros((half_y, slots), f32)
    for j in range(rank_rows):
        below = below + jnp.where(tile_ranks[:, j : j + 1] < slot_rank, 1.0, 0.0)
    place = jnp.sum(below, axis=0, keepdims=True).astype(jnp.int32)
    owner, nth = lax.div(place, per_device), lax.rem(place, per_device)
    line = lax.div(nth, rows) * LANES + lax.rem(nth, rows) * devices + owner
    line = jnp.where(listed, line, -1)
    order = hot_rows(slots, line)
    own_rank = lax.rem(slot_rank.astype(jnp.int32), owned)
    own_high = lax.shift_right_logical(own_rank, 8).astype(f32)
    own_low = lax.bitwise_and(own_rank, 255).astype(f32)
    rank_table = jnp.concatenate(
        [jnp.broadcast_to(own, (LANES, slots)).astype(bf16) for own in (own_high, own_low)],
        axis=0,
    )
    rank_lines = lax.dot_general(
        order, rank_table, (((1,), (1,)), ((), ())), preferred_element_type=f32
    )
    rank_lines = 256.0 * rank_lines[:, :LANES] + rank_lines[:, LANES:]
    lane_group = lax.div(iota((LANES, LANES), 1), DL)
    rank_block = jnp.zeros((LANES, LANES), f32)
    for j in range(groups):
        rank_block = jnp.where(
            lane_group == j, rank_lines[j * LANES : (j + 1) * LANES], rank_block
        )

    loads[2].wait()
    loads[4].wait()
    loads[5].wait()
    batch = 256 // cy

    def add_cells(g, carry):
        slot_parts, parts = [], []
        for a in range(batch):
            x = g * batch + a
            slot_parts.append(cs_v[pl.ds(x, 1), :])
            density = e_v[0, x].astype(f32) * f_v[0, x].astype(f32)
            for c in (1, 2):
                density = density + e_v[c, x].astype(f32) * f_v[c, x].astype(f32)
            parts.append(jnp.concatenate(split(density), axis=1))
        cell_slots = jnp.concatenate(slot_parts, axis=1)
        hot = hot_rows(slots, cell_slots)
        acc[...] += dot(hot, jnp.concatenate(parts, axis=0))
        return carry

    acc[...] = jnp.zeros_like(acc)
    lax.fori_loop(0, cx // batch, add_cells, 0, unroll=2)
    loads[3].wait()

    def gather_rows(x, carry):
        for c in range(3):
            first = e_v[c, x, 0:16, :].astype(f32)
            last = e_v[c, x, cy - 16 : cy, :].astype(f32)
            stage[c, pl.ds(x, 1), :] = first[0:1]
            stage[3 + c, pl.ds(x, 1), :] = last[15:16]
        for k, c in enumerate((0, 2)):
            stage[6 + k, pl.ds(x, 1), :] = h_v[c, x, cy - 16 : cy, :].astype(f32)[15:16]
        return carry

    lax.fori_loop(0, cx, gather_rows, 0, unroll=4)
    out_y_prev[0] = stage[0].astype(bf16)
    out_y_prev[1] = stage[2].astype(bf16)
    for k in range(5):
        out_y_next[k] = stage[3 + k].astype(bf16)

    pl.semaphore_wait(barrier, devices - 1)

    faces = [
        (e_hbm.at[pl.ds(1, 2), 0], in_xn, -1, 0),
        (out_y_prev, in_yn, 0, -1),
        (e_hbm.at[:, cx - 1], in_xpe, 1, 0),
        (h_hbm.at[pl.ds(1, 2), cx - 1], in_xph, 1, 0),
        (out_y_next, in_yp, 0, 1),
        (e_hbm.at[0, cx - 1, pl.ds(0, 16)], in_c1, 1, -1),
        (e_hbm.at[1, 0, pl.ds(cy - 16, 16)], in_c2, -1, 1),
    ]

    def inside(step_x, step_y):
        there = None
        for at, step, count in ((gx, step_x, count_x), (gy, step_y, count_y)):
            if step:
                fits = at + step < count if step > 0 else at + step >= 0
                there = fits if there is None else jnp.logical_and(there, fits)
        return there

    def face_copy(i):
        source, landing, step_x, step_y = faces[i]
        return pltpu.make_async_remote_copy(
            src_ref=source,
            dst_ref=landing,
            send_sem=face_send.at[i],
            recv_sem=face_recv.at[i],
            device_id=(gx + step_x, gy + step_y),
            device_id_type=MESH,
        )

    for i, (_, landing, step_x, step_y) in enumerate(faces):

        @pl.when(inside(step_x, step_y))
        def _():
            face_copy(i).start()

        @pl.when(jnp.logical_not(inside(-step_x, -step_y)))
        def _():
            landing[...] = jnp.zeros(landing.shape, landing.dtype)

    sums = acc[:, :nz] + acc[:, nz:]
    sorted_sums = dot(order, jnp.concatenate(split(sums), axis=1)).astype(bf16)
    packed = jnp.concatenate(
        [
            jnp.concatenate(
                [
                    sorted_sums[j * LANES : (j + 1) * LANES, half * nz : (half + 1) * nz]
                    for j in range(groups)
                ],
                axis=1,
            )
            for half in range(2)
        ],
        axis=0,
    )
    layer = lax.div(iota((nz, LANES), 0), nz // DL)
    lane = iota((nz, LANES), 1)
    pool = jnp.concatenate([one_hot(layer + j * DL == lane) for j in range(groups)], axis=0)
    pooled = dot(packed, pool)
    pooled = pooled[:LANES] + pooled[LANES:]
    if 2 * rows < BLOCK:
        send[...] = jnp.zeros_like(send)
    for i in range(rows):
        part = slice(i * devices, (i + 1) * devices)
        send[pl.ds(i, devices, stride=BLOCK), :] = pooled[part]
        send[pl.ds(rows + i, devices, stride=BLOCK), :] = rank_block[part]

    mine = pl.ds(pl.multiple_of(me * BLOCK, BLOCK), BLOCK)

    def send_part(step, carry):
        device, where = partner(step)
        pltpu.make_async_remote_copy(
            src_ref=send.at[pl.ds(pl.multiple_of(device * BLOCK, BLOCK), BLOCK)],
            dst_ref=recv.at[mine],
            send_sem=part_send,
            recv_sem=part_recv,
            device_id=where,
            device_id_type=MESH,
        ).start()
        return carry

    lax.fori_loop(1, devices, send_part, 0)
    recv[mine, :] = send[mine, :]

    for i, (_, _, step_x, step_y) in enumerate(faces):

        @pl.when(inside(-step_x, -step_y))
        def _():
            face_copy(i).wait_recv()

    for c in (1, 2):
        e_v[c, cx] = in_xn[c - 1]
    for k in range(2):
        yn[k] = in_yn[k].astype(f32)

    pe_x, pe_y, pe_z, ph_x, ph_z = [in_yp[k].astype(f32) for k in range(5)]
    first_x, first_z = stage[0], stage[2]
    edge_x = ph_x - courant * ((first_z - pe_z) - (next_z(pe_y) - pe_y))
    corner = in_c2[...].astype(f32)[15:16]
    edge_z = ph_z - courant * ((next_row(pe_y, corner) - pe_y) - (first_x - pe_x))
    keep_y = gy > 0
    hy_edge[0] = jnp.where(keep_y, edge_x, 0.0).astype(bf16).astype(f32)
    hy_edge[1] = jnp.where(keep_y, edge_z, 0.0).astype(bf16).astype(f32)

    pe_x, pe_y, pe_z = [in_xpe[k].astype(f32) for k in range(3)]
    ph_y, ph_z = [in_xph[k].astype(f32) for k in range(2)]
    first_y, first_z = e_v[1, 0].astype(f32), e_v[2, 0].astype(f32)
    back_y = ph_y - courant * ((next_z(pe_x) - pe_x) - (first_z - pe_z))
    corner = in_c1[...].astype(f32)[0:1]
    back_z = ph_z - courant * ((first_y - pe_y) - (next_row(pe_x, corner) - pe_x))
    keep_x = gx > 0
    hx_edge[0] = jnp.where(keep_x, back_y, 0.0).astype(bf16)
    hx_edge[1] = jnp.where(keep_x, back_z, 0.0).astype(bf16)

    def update_h(x, carry):
        e_x, e_y, e_z = [e_v[c, x].astype(f32) for c in range(3)]
        nx_y, nx_z = [e_v[c, x + 1].astype(f32) for c in (1, 2)]
        ny_x, ny_z = [yn[k, pl.ds(x, 1), :] for k in range(2)]
        d_y_z, d_z_y = next_row(e_z, ny_z) - e_z, next_z(e_y) - e_y
        nh[0, x] = (h_v[0, x].astype(f32) - courant * (d_y_z - d_z_y)).astype(bf16)
        d_z_x, d_x_z = next_z(e_x) - e_x, nx_z - e_z
        nh[1, x] = (h_v[1, x].astype(f32) - courant * (d_z_x - d_x_z)).astype(bf16)
        d_x_y, d_y_x = nx_y - e_y, next_row(e_x, ny_x) - e_x
        nh[2, x] = (h_v[2, x].astype(f32) - courant * (d_x_y - d_y_x)).astype(bf16)
        return carry

    lax.fori_loop(0, cx, update_h, 0, unroll=4)

    loads[6].wait()
    loads[7].wait()
    materials = eps_v.shape[0]
    factors = [courant * eps_v[k] for k in range(materials)]

    def update_e(x, carry):
        back_y, back_z = [value.astype(f32) for value in carry]
        ahead = nh[1, x], nh[2, x]
        h_x = nh[0, x].astype(f32)
        h_y, h_z = [value.astype(f32) for value in ahead]
        before_x, before_z = [hy_edge[k, pl.ds(x, 1), :] for k in range(2)]
        material = m_v[x]
        factor = jnp.full(material.shape, factors[-1], f32)
        for which in range(materials - 1):
            factor = jnp.where(material == which, factors[which], factor)
        b_y_z, b_z_y = h_z - prior_row(h_z, before_z), h_y - prior_z(h_y)
        ne[0, x] = (e_v[0, x].astype(f32) + factor * (b_y_z - b_z_y)).astype(bf16)
        b_z_x, b_x_z = h_x - prior_z(h_x), h_z - back_z
        ne[1, x] = (e_v[1, x].astype(f32) + factor * (b_z_x - b_x_z)).astype(bf16)
        b_x_y, b_y_x = h_y - back_y, h_x - prior_row(h_x, before_x)
        ne[2, x] = (e_v[2, x].astype(f32) + factor * (b_x_y - b_y_x)).astype(bf16)
        return ahead

    lax.fori_loop(0, cx, update_e, (hx_edge[0], hx_edge[1]), unroll=4)

    others = pl.ds(0, (devices - 1) * BLOCK)
    arrivals = pltpu.make_async_remote_copy(
        src_ref=send.at[others],
        dst_ref=recv.at[others],
        send_sem=part_send,
        recv_sem=part_recv,
        device_id=(gx, gy),
        device_id_type=MESH,
    )
    arrivals.wait_recv()
    arrivals.wait_send()
    for i, (_, _, step_x, step_y) in enumerate(faces):

        @pl.when(inside(step_x, step_y))
        def _():
            face_copy(i).wait_send()


def finish(
    ne_v,
    nh_v,
    recv,
    ne,
    nh,
    grad,
    grad_v,
    store_sem,
):
    devices = recv.shape[0] // BLOCK
    owned = grad.shape[1]
    groups = LANES // DL
    rows = owned // devices // groups

    stores = [
        pltpu.make_async_copy(src, dst, store_sem.at[i])
        for i, (src, dst) in enumerate([(ne_v, ne), (nh_v, nh), (grad_v, grad)])
    ]
    stores[0].start()
    stores[1].start()

    values = jnp.concatenate(
        [recv[pl.ds(i, devices, stride=BLOCK), :] for i in range(rows)], axis=0
    )
    value_ranks = jnp.concatenate(
        [recv[pl.ds(rows + i, devices, stride=BLOCK), :] for i in range(rows)], axis=0
    )
    turned_values = values.T
    terms = jnp.concatenate(
        [turned_values[j * DL : (j + 1) * DL] for j in range(groups)], axis=1
    )
    lane_rank = iota((LANES, owned), 1).astype(f32)
    target = jnp.concatenate(
        [one_hot(value_ranks[:, j * DL : j * DL + 1] == lane_rank) for j in range(groups)],
        axis=0,
    )
    result = dot(jnp.concatenate(split(terms), axis=0), target)
    grad_v[...] = grad_scale * (result[:DL] + result[DL:])

    stores[2].start()
    for store in stores:
        store.wait()


def per_device(
    adjoint_e, adjoint_h, material, inv_eps, forward_design, cell_slot, tile_pillars, pillar_rank
):
    count_x, count_y = lax.axis_size("gx"), lax.axis_size("gy")
    devices = count_x * count_y
    _, cx, cy, nz = adjoint_e.shape
    slots = tile_pillars.shape[2]
    ranks = pillar_rank.reshape(-1, LANES)
    rank_rows = ranks.shape[0] // count_x
    owned = pillar_rank.shape[0] // devices
    anywhere = pl.BlockSpec(memory_space=pl.ANY)
    vmem = pl.BlockSpec(memory_space=pltpu.VMEM)
    operands = [
        pltpu.with_memory_space_constraint(operand, pltpu.HBM)
        for operand in (
            adjoint_e,
            adjoint_h,
            material,
            inv_eps,
            forward_design,
            cell_slot,
            tile_pillars,
            ranks,
        )
    ]
    kept = pl.pallas_call(
        functools.partial(exchange, count_x, count_y),
        out_shape=(
            pltpu.VMEM((3, cx, cy, nz), bf16),
            pltpu.VMEM((3, cx, cy, nz), bf16),
            pltpu.VMEM((devices * BLOCK, LANES), f32),
        ),
        in_specs=[anywhere] * 8,
        out_specs=(vmem,) * 3,
        scratch_shapes=[
            pltpu.VMEM((3, cx + 1, cy, nz), bf16),
            pltpu.VMEM((cx, cy, nz), jnp.int32),
            pltpu.VMEM((2, cy, nz), bf16),
            pltpu.VMEM((2, cx, nz), f32),
            pltpu.VMEM((3, cx, cy, nz), bf16),
            pltpu.VMEM((3, cx, cy, nz), bf16),
            pltpu.SMEM(inv_eps.shape, f32),
            pltpu.VMEM((cx, cy), jnp.int32),
            pltpu.VMEM((count_y, slots), jnp.int32),
            pltpu.VMEM((rank_rows, LANES), jnp.int32),
            pltpu.VMEM((LANES, LANES), f32),
            pltpu.VMEM((slots, 2 * nz), f32),
            pltpu.VMEM((8, cx, nz), f32),
            pltpu.VMEM((2, cx, nz), bf16),
            pltpu.VMEM((5, cx, nz), bf16),
            pltpu.VMEM((2, cy, nz), bf16),
            pltpu.VMEM((3, cy, nz), bf16),
            pltpu.VMEM((2, cy, nz), bf16),
            pltpu.VMEM((2, cx, nz), bf16),
            pltpu.VMEM((5, cx, nz), bf16),
            pltpu.VMEM((16, nz), bf16),
            pltpu.VMEM((16, nz), bf16),
            pltpu.VMEM((2, cx, nz), f32),
            pltpu.VMEM((devices * BLOCK, LANES), f32),
            pltpu.SemaphoreType.DMA((8,)),
            pltpu.SemaphoreType.DMA((7,)),
            pltpu.SemaphoreType.DMA((7,)),
            pltpu.SemaphoreType.DMA,
            pltpu.SemaphoreType.DMA,
        ],
        compiler_params=pltpu.CompilerParams(
            collective_id=0, has_side_effects=True, vmem_limit_bytes=24 * 1024 * 1024
        ),
    )(*operands)
    return pl.pallas_call(
        finish,
        out_shape=(
            pltpu.HBM(adjoint_e.shape, bf16),
            pltpu.HBM(adjoint_h.shape, bf16),
            pltpu.HBM((DL, owned), f32),
        ),
        in_specs=[vmem] * 3,
        out_specs=(anywhere,) * 3,
        scratch_shapes=[
            pltpu.VMEM((DL, owned), f32),
            pltpu.SemaphoreType.DMA((3,)),
        ],
        compiler_params=pltpu.CompilerParams(vmem_limit_bytes=16 * 1024 * 1024),
    )(*[pltpu.with_memory_space_constraint(value, pltpu.VMEM) for value in kept])


def solution(mesh):
    return jax.shard_map(
        per_device,
        mesh=mesh,
        in_specs=(
            P(None, "gx", "gy", None),
            P(None, "gx", "gy", None),
            P("gx", "gy", None),
            P(),
            P(None, "gx", "gy", None),
            P("gx", "gy"),
            P(),
            P(),
        ),
        out_specs=(P(None, "gx", "gy", None), P(None, "gx", "gy", None), P(None, ("gx", "gy"))),
        check_vma=False,
    )
```

```python
import functools

import jax
import jax.numpy as jnp
from jax import lax
from jax.experimental import pallas as pl
from jax.experimental.pallas import tpu as pltpu
from jax.sharding import PartitionSpec as P

DL = 32

courant = 0.5
grad_scale = 0.125

MESH = pl.DeviceIdType.MESH
f32 = jnp.float32
bf16 = jnp.bfloat16
LANES = 128
BLOCK = 8


def iota(shape, axis):
    return lax.broadcasted_iota(jnp.int32, shape, axis)


def dot(a, b):
    return jnp.dot(a, b, preferred_element_type=f32)


def one_hot(mask):
    return jnp.where(mask, 1.0, 0.0).astype(bf16)


def hot_rows(count, row):
    size = row.shape[1]
    number = iota((count, size), 0).astype(jnp.int16).reshape(count // 16, 16, size)
    entry = jnp.broadcast_to(row, (16, size)).astype(jnp.int16)
    hot = jnp.where(number == entry[None], jnp.ones((), bf16), jnp.zeros((), bf16))
    return hot.reshape(count, size)


def split(value):
    high = value.astype(bf16)
    return high, (value - high.astype(f32)).astype(bf16)


def next_z(field):
    size = field.shape[1]
    return jnp.where(iota((1, size), 1) == size - 1, 0.0, pltpu.roll(field, size - 1, 1))


def prior_z(field):
    return jnp.where(iota((1, field.shape[1]), 1) == 0, 0.0, pltpu.roll(field, 1, 1))


def next_row(field, edge):
    size = field.shape[0]
    return jnp.where(iota((size, 1), 0) == size - 1, edge, pltpu.roll(field, size - 1, 0))


def prior_row(field, edge):
    return jnp.where(iota((field.shape[0], 1), 0) == 0, edge, pltpu.roll(field, 1, 0))


def exchange(
    count_x,
    count_y,
    e_hbm,
    h_hbm,
    m_hbm,
    eps_hbm,
    f_hbm,
    cs_hbm,
    tp_hbm,
    pr_hbm,
    ne,
    nh,
    recv,
    e_v,
    m_v,
    hy_edge,
    h_v,
    f_v,
    eps_v,
    cs_v,
    tp_v,
    pr_v,
    rt_v,
    acc,
    stage,
    out_y_prev,
    out_y_next,
    in_xn,
    in_xpe,
    in_xph,
    in_yn,
    in_yp,
    in_c1,
    in_c2,
    yn,
    send,
    load_sem,
    face_send,
    face_recv,
    part_send,
    part_recv,
):
    _, cx, cy, nz = e_hbm.shape
    slots = tp_hbm.shape[2]
    devices = count_x * count_y
    half_x, half_y = cx // 2, cy // 2
    width = count_y * half_y
    rank_rows = pr_v.shape[0]
    per_device = slots // devices
    groups = LANES // DL
    rows = per_device // groups
    owned = pr_hbm.shape[0] * LANES // devices

    gx, gy = lax.axis_index("gx"), lax.axis_index("gy")
    me = gx * count_y + gy

    loads = [
        pltpu.make_async_copy(src, dst, load_sem.at[i])
        for i, (src, dst) in enumerate(
            [
                (tp_hbm.at[gx], tp_v),
                (pr_hbm.at[pl.ds(pl.multiple_of(gx * rank_rows, 8), rank_rows)], pr_v),
                (e_hbm, e_v.at[:, pl.ds(0, cx)]),
                (h_hbm, h_v),
                (cs_hbm, cs_v),
                (f_hbm, f_v),
                (eps_hbm, eps_v),
                (m_hbm, m_v),
            ]
        )
    ]
    for load in loads:
        load.start()

    barrier = pltpu.get_barrier_semaphore()

    def partner(step):
        device = lax.rem(me + step, devices)
        return device, (lax.div(device, count_y), lax.rem(device, count_y))

    def greet(step, carry):
        pl.semaphore_signal(barrier, inc=1, device_id=partner(step)[1], device_id_type=MESH)
        return carry

    lax.fori_loop(1, devices, greet, 0)

    loads[0].wait()
    loads[1].wait()
    tile_row = iota(tp_v.shape, 0) == gy
    ids = jnp.sum(jnp.where(tile_row, tp_v[...], 0), axis=0, keepdims=True)
    listed = ids >= 0
    local = jnp.where(listed, ids - gx * (half_x * width), 0)
    local_row, local_lane = lax.div(local, LANES), lax.rem(local, LANES)
    ranks = pr_v[...]
    if rank_rows < LANES:
        ranks = jnp.concatenate(
            [ranks, jnp.zeros((LANES - rank_rows, LANES), jnp.int32)], axis=0
        )
    turned_high = lax.shift_right_logical(ranks, 8).astype(f32).T
    turned_low = lax.bitwise_and(ranks, 255).astype(f32).T
    table = jnp.concatenate([turned_high.astype(bf16), turned_low.astype(bf16)], axis=0)
    picked = dot(table, one_hot(iota((LANES, slots), 0) == local_row))
    picked = 256.0 * picked[:LANES] + picked[LANES:]
    slot_rank = jnp.sum(
        jnp.where(iota((LANES, slots), 0) == local_lane, picked, 0.0), axis=0, keepdims=True
    )
    turned = 256.0 * turned_high + turned_low
    along_y = lax.rem(iota((LANES, LANES), 1) * LANES + iota((LANES, LANES), 0), width)
    rt_v[...] = jnp.where(lax.div(along_y, half_y) == gy, turned, 1e9)
    tile_ranks = rt_v[
        pl.ds(pl.multiple_of(lax.rem(gy * half_y, LANES), half_y), half_y), :
    ]
    below = jnp.zeros((half_y, slots), f32)
    for j in range(rank_rows):
        below = below + jnp.where(tile_ranks[:, j : j + 1] < slot_rank, 1.0, 0.0)
    place = jnp.sum(below, axis=0, keepdims=True).astype(jnp.int32)
    owner, nth = lax.div(place, per_device), lax.rem(place, per_device)
    line = lax.div(nth, rows) * LANES + lax.rem(nth, rows) * devices + owner
    line = jnp.where(listed, line, -1)
    order = hot_rows(slots, line)
    own_rank = lax.rem(slot_rank.astype(jnp.int32), owned)
    own_high = lax.shift_right_logical(own_rank, 8).astype(f32)
    own_low = lax.bitwise_and(own_rank, 255).astype(f32)
    rank_table = jnp.concatenate(
        [jnp.broadcast_to(own, (LANES, slots)).astype(bf16) for own in (own_high, own_low)],
        axis=0,
    )
    rank_lines = lax.dot_general(
        order, rank_table, (((1,), (1,)), ((), ())), preferred_element_type=f32
    )
    rank_lines = 256.0 * rank_lines[:, :LANES] + rank_lines[:, LANES:]
    lane_group = lax.div(iota((LANES, LANES), 1), DL)
    rank_block = jnp.zeros((LANES, LANES), f32)
    for j in range(groups):
        rank_block = jnp.where(
            lane_group == j, rank_lines[j * LANES : (j + 1) * LANES], rank_block
        )

    loads[2].wait()
    loads[4].wait()
    loads[5].wait()
    batch = 256 // cy

    def add_cells(g, carry):
        slot_parts, parts = [], []
        for a in range(batch):
            x = g * batch + a
            slot_parts.append(cs_v[pl.ds(x, 1), :])
            density = e_v[0, x].astype(f32) * f_v[0, x].astype(f32)
            for c in (1, 2):
                density = density + e_v[c, x].astype(f32) * f_v[c, x].astype(f32)
            parts.append(jnp.concatenate(split(density), axis=1))
        cell_slots = jnp.concatenate(slot_parts, axis=1)
        hot = hot_rows(slots, cell_slots)
        acc[...] += dot(hot, jnp.concatenate(parts, axis=0))
        return carry

    acc[...] = jnp.zeros_like(acc)
    lax.fori_loop(0, cx // batch, add_cells, 0, unroll=2)
    loads[3].wait()

    def gather_rows(x, carry):
        for c in range(3):
            first = e_v[c, x, 0:16, :].astype(f32)
            last = e_v[c, x, cy - 16 : cy, :].astype(f32)
            stage[c, pl.ds(x, 1), :] = first[0:1]
            stage[3 + c, pl.ds(x, 1), :] = last[15:16]
        for k, c in enumerate((0, 2)):
            stage[6 + k, pl.ds(x, 1), :] = h_v[c, x, cy - 16 : cy, :].astype(f32)[15:16]
        return carry

    lax.fori_loop(0, cx, gather_rows, 0, unroll=4)
    out_y_prev[0] = stage[0].astype(bf16)
    out_y_prev[1] = stage[2].astype(bf16)
    for k in range(5):
        out_y_next[k] = stage[3 + k].astype(bf16)

    pl.semaphore_wait(barrier, devices - 1)

    faces = [
        (out_y_prev, in_yn, 0, -1),
        (out_y_next, in_yp, 0, 1),
        (e_hbm.at[1, 0, pl.ds(cy - 16, 16)], in_c2, -1, 1),
        (e_hbm.at[pl.ds(1, 2), 0], in_xn, -1, 0),
        (e_hbm.at[:, cx - 1], in_xpe, 1, 0),
        (h_hbm.at[pl.ds(1, 2), cx - 1], in_xph, 1, 0),
        (e_hbm.at[0, cx - 1, pl.ds(0, 16)], in_c1, 1, -1),
    ]

    def inside(step_x, step_y):
        there = None
        for at, step, count in ((gx, step_x, count_x), (gy, step_y, count_y)):
            if step:
                fits = at + step < count if step > 0 else at + step >= 0
                there = fits if there is None else jnp.logical_and(there, fits)
        return there

    def face_copy(i):
        source, landing, step_x, step_y = faces[i]
        return pltpu.make_async_remote_copy(
            src_ref=source,
            dst_ref=landing,
            send_sem=face_send.at[i],
            recv_sem=face_recv.at[i],
            device_id=(gx + step_x, gy + step_y),
            device_id_type=MESH,
        )

    for i, (_, landing, step_x, step_y) in enumerate(faces):

        @pl.when(inside(step_x, step_y))
        def _():
            face_copy(i).start()

        @pl.when(jnp.logical_not(inside(-step_x, -step_y)))
        def _():
            landing[...] = jnp.zeros(landing.shape, landing.dtype)

    sums = acc[:, :nz] + acc[:, nz:]
    sorted_sums = dot(order, jnp.concatenate(split(sums), axis=1)).astype(bf16)
    packed = jnp.concatenate(
        [
            jnp.concatenate(
                [
                    sorted_sums[j * LANES : (j + 1) * LANES, half * nz : (half + 1) * nz]
                    for j in range(groups)
                ],
                axis=1,
            )
            for half in range(2)
        ],
        axis=0,
    )
    layer = lax.div(iota((nz, LANES), 0), nz // DL)
    lane = iota((nz, LANES), 1)
    pool = jnp.concatenate([one_hot(layer + j * DL == lane) for j in range(groups)], axis=0)
    pooled = dot(packed, pool)
    pooled = pooled[:LANES] + pooled[LANES:]
    if 2 * rows < BLOCK:
        send[...] = jnp.zeros_like(send)
    for i in range(rows):
        part = slice(i * devices, (i + 1) * devices)
        send[pl.ds(i, devices, stride=BLOCK), :] = pooled[part]
        send[pl.ds(rows + i, devices, stride=BLOCK), :] = rank_block[part]

    mine = pl.ds(pl.multiple_of(me * BLOCK, BLOCK), BLOCK)

    def send_part(step, carry):
        device, where = partner(step)
        pltpu.make_async_remote_copy(
            src_ref=send.at[pl.ds(pl.multiple_of(device * BLOCK, BLOCK), BLOCK)],
            dst_ref=recv.at[mine],
            send_sem=part_send,
            recv_sem=part_recv,
            device_id=where,
            device_id_type=MESH,
        ).start()
        return carry

    lax.fori_loop(1, devices, send_part, 0)
    recv[mine, :] = send[mine, :]

    def await_faces(which):
        for i in which:

            @pl.when(inside(-faces[i][2], -faces[i][3]))
            def _():
                face_copy(i).wait_recv()

    await_faces([0])
    for k in range(2):
        yn[k] = in_yn[k].astype(f32)

    def update_h(x, carry):
        e_x, e_y, e_z = [e_v[c, x].astype(f32) for c in range(3)]
        nx_y, nx_z = [e_v[c, x + 1].astype(f32) for c in (1, 2)]
        ny_x, ny_z = [yn[k, pl.ds(x, 1), :] for k in range(2)]
        d_y_z, d_z_y = next_row(e_z, ny_z) - e_z, next_z(e_y) - e_y
        nh[0, x] = (h_v[0, x].astype(f32) - courant * (d_y_z - d_z_y)).astype(bf16)
        d_z_x, d_x_z = next_z(e_x) - e_x, nx_z - e_z
        nh[1, x] = (h_v[1, x].astype(f32) - courant * (d_z_x - d_x_z)).astype(bf16)
        d_x_y, d_y_x = nx_y - e_y, next_row(e_x, ny_x) - e_x
        nh[2, x] = (h_v[2, x].astype(f32) - courant * (d_x_y - d_y_x)).astype(bf16)
        return carry

    unrolled = 4
    main = (cx - 1) // unrolled * unrolled
    lax.fori_loop(0, main, update_h, 0, unroll=unrolled)
    for x in range(main, cx - 1):
        update_h(x, 0)
    await_faces([3])
    for c in (1, 2):
        e_v[c, cx] = in_xn[c - 1]
    update_h(cx - 1, 0)

    await_faces([1, 2])
    pe_x, pe_y, pe_z, ph_x, ph_z = [in_yp[k].astype(f32) for k in range(5)]
    first_x, first_z = stage[0], stage[2]
    edge_x = ph_x - courant * ((first_z - pe_z) - (next_z(pe_y) - pe_y))
    corner = in_c2[...].astype(f32)[15:16]
    edge_z = ph_z - courant * ((next_row(pe_y, corner) - pe_y) - (first_x - pe_x))
    keep_y = gy > 0
    hy_edge[0] = jnp.where(keep_y, edge_x, 0.0).astype(bf16).astype(f32)
    hy_edge[1] = jnp.where(keep_y, edge_z, 0.0).astype(bf16).astype(f32)

    loads[6].wait()
    loads[7].wait()
    materials = eps_v.shape[0]
    factors = [courant * eps_v[k] for k in range(materials)]

    def update_e(x, carry):
        back_y, back_z = [value.astype(f32) for value in carry]
        ahead = nh[1, x], nh[2, x]
        h_x = nh[0, x].astype(f32)
        h_y, h_z = [value.astype(f32) for value in ahead]
        before_x, before_z = [hy_edge[k, pl.ds(x, 1), :] for k in range(2)]
        material = m_v[x]
        factor = jnp.full(material.shape, factors[-1], f32)
        for which in range(materials - 1):
            factor = jnp.where(material == which, factors[which], factor)
        b_y_z, b_z_y = h_z - prior_row(h_z, before_z), h_y - prior_z(h_y)
        ne[0, x] = (e_v[0, x].astype(f32) + factor * (b_y_z - b_z_y)).astype(bf16)
        b_z_x, b_x_z = h_x - prior_z(h_x), h_z - back_z
        ne[1, x] = (e_v[1, x].astype(f32) + factor * (b_z_x - b_x_z)).astype(bf16)
        b_x_y, b_y_x = h_y - back_y, h_x - prior_row(h_x, before_x)
        ne[2, x] = (e_v[2, x].astype(f32) + factor * (b_x_y - b_y_x)).astype(bf16)
        return ahead

    carry = nh[1, 0], nh[2, 0]
    carry = lax.fori_loop(1, 1 + main, update_e, carry, unroll=unrolled)
    for x in range(1 + main, cx):
        carry = update_e(x, carry)

    await_faces([4, 5, 6])
    pe_x, pe_y, pe_z = [in_xpe[k].astype(f32) for k in range(3)]
    ph_y, ph_z = [in_xph[k].astype(f32) for k in range(2)]
    first_y, first_z = e_v[1, 0].astype(f32), e_v[2, 0].astype(f32)
    back_y = ph_y - courant * ((next_z(pe_x) - pe_x) - (first_z - pe_z))
    corner = in_c1[...].astype(f32)[0:1]
    back_z = ph_z - courant * ((first_y - pe_y) - (next_row(pe_x, corner) - pe_x))
    keep_x = gx > 0
    edge_y = jnp.where(keep_x, back_y, 0.0).astype(bf16)
    edge_z = jnp.where(keep_x, back_z, 0.0).astype(bf16)

    update_e(0, (edge_y, edge_z))

    others = pl.ds(0, (devices - 1) * BLOCK)
    arrivals = pltpu.make_async_remote_copy(
        src_ref=send.at[others],
        dst_ref=recv.at[others],
        send_sem=part_send,
        recv_sem=part_recv,
        device_id=(gx, gy),
        device_id_type=MESH,
    )
    arrivals.wait_recv()
    arrivals.wait_send()
    for i, (_, _, step_x, step_y) in enumerate(faces):

        @pl.when(inside(step_x, step_y))
        def _():
            face_copy(i).wait_send()


def finish(
    ne_v,
    nh_v,
    recv,
    ne,
    nh,
    grad,
    grad_v,
    store_sem,
):
    devices = recv.shape[0] // BLOCK
    owned = grad.shape[1]
    groups = LANES // DL
    rows = owned // devices // groups

    stores = [
        pltpu.make_async_copy(src, dst, store_sem.at[i])
        for i, (src, dst) in enumerate([(ne_v, ne), (nh_v, nh), (grad_v, grad)])
    ]
    stores[0].start()
    stores[1].start()

    values = jnp.concatenate(
        [recv[pl.ds(i, devices, stride=BLOCK), :] for i in range(rows)], axis=0
    )
    value_ranks = jnp.concatenate(
        [recv[pl.ds(rows + i, devices, stride=BLOCK), :] for i in range(rows)], axis=0
    )
    turned_values = values.T
    terms = jnp.concatenate(
        [turned_values[j * DL : (j + 1) * DL] for j in range(groups)], axis=1
    )
    lane_rank = iota((LANES, owned), 1).astype(f32)
    target = jnp.concatenate(
        [one_hot(value_ranks[:, j * DL : j * DL + 1] == lane_rank) for j in range(groups)],
        axis=0,
    )
    result = dot(jnp.concatenate(split(terms), axis=0), target)
    grad_v[...] = grad_scale * (result[:DL] + result[DL:])

    stores[2].start()
    for store in stores:
        store.wait()


def per_device(
    adjoint_e, adjoint_h, material, inv_eps, forward_design, cell_slot, tile_pillars, pillar_rank
):
    count_x, count_y = lax.axis_size("gx"), lax.axis_size("gy")
    devices = count_x * count_y
    _, cx, cy, nz = adjoint_e.shape
    slots = tile_pillars.shape[2]
    ranks = pillar_rank.reshape(-1, LANES)
    rank_rows = ranks.shape[0] // count_x
    owned = pillar_rank.shape[0] // devices
    anywhere = pl.BlockSpec(memory_space=pl.ANY)
    vmem = pl.BlockSpec(memory_space=pltpu.VMEM)
    operands = [
        pltpu.with_memory_space_constraint(operand, pltpu.HBM)
        for operand in (
            adjoint_e,
            adjoint_h,
            material,
            inv_eps,
            forward_design,
            cell_slot,
            tile_pillars,
            ranks,
        )
    ]
    kept = pl.pallas_call(
        functools.partial(exchange, count_x, count_y),
        out_shape=(
            pltpu.VMEM((3, cx, cy, nz), bf16),
            pltpu.VMEM((3, cx, cy, nz), bf16),
            pltpu.VMEM((devices * BLOCK, LANES), f32),
        ),
        in_specs=[anywhere] * 8,
        out_specs=(vmem,) * 3,
        scratch_shapes=[
            pltpu.VMEM((3, cx + 1, cy, nz), bf16),
            pltpu.VMEM((cx, cy, nz), jnp.int32),
            pltpu.VMEM((2, cx, nz), f32),
            pltpu.VMEM((3, cx, cy, nz), bf16),
            pltpu.VMEM((3, cx, cy, nz), bf16),
            pltpu.SMEM(inv_eps.shape, f32),
            pltpu.VMEM((cx, cy), jnp.int32),
            pltpu.VMEM((count_y, slots), jnp.int32),
            pltpu.VMEM((rank_rows, LANES), jnp.int32),
            pltpu.VMEM((LANES, LANES), f32),
            pltpu.VMEM((slots, 2 * nz), f32),
            pltpu.VMEM((8, cx, nz), f32),
            pltpu.VMEM((2, cx, nz), bf16),
            pltpu.VMEM((5, cx, nz), bf16),
            pltpu.VMEM((2, cy, nz), bf16),
            pltpu.VMEM((3, cy, nz), bf16),
            pltpu.VMEM((2, cy, nz), bf16),
            pltpu.VMEM((2, cx, nz), bf16),
            pltpu.VMEM((5, cx, nz), bf16),
            pltpu.VMEM((16, nz), bf16),
            pltpu.VMEM((16, nz), bf16),
            pltpu.VMEM((2, cx, nz), f32),
            pltpu.VMEM((devices * BLOCK, LANES), f32),
            pltpu.SemaphoreType.DMA((8,)),
            pltpu.SemaphoreType.DMA((7,)),
            pltpu.SemaphoreType.DMA((7,)),
            pltpu.SemaphoreType.DMA,
            pltpu.SemaphoreType.DMA,
        ],
        compiler_params=pltpu.CompilerParams(
            collective_id=0, has_side_effects=True, vmem_limit_bytes=24 * 1024 * 1024
        ),
    )(*operands)
    return pl.pallas_call(
        finish,
        out_shape=(
            pltpu.HBM(adjoint_e.shape, bf16),
            pltpu.HBM(adjoint_h.shape, bf16),
            pltpu.HBM((DL, owned), f32),
        ),
        in_specs=[vmem] * 3,
        out_specs=(anywhere,) * 3,
        scratch_shapes=[
            pltpu.VMEM((DL, owned), f32),
            pltpu.SemaphoreType.DMA((3,)),
        ],
        compiler_params=pltpu.CompilerParams(vmem_limit_bytes=16 * 1024 * 1024),
    )(*[pltpu.with_memory_space_constraint(value, pltpu.VMEM) for value in kept])


def solution(mesh):
    return jax.shard_map(
        per_device,
        mesh=mesh,
        in_specs=(
            P(None, "gx", "gy", None),
            P(None, "gx", "gy", None),
            P("gx", "gy", None),
            P(),
            P(None, "gx", "gy", None),
            P("gx", "gy"),
            P(),
            P(),
        ),
        out_specs=(P(None, "gx", "gy", None), P(None, "gx", "gy", None), P(None, ("gx", "gy"))),
        check_vma=False,
    )
```

```python
import functools

import jax
import jax.numpy as jnp
from jax import lax
from jax.experimental import pallas as pl
from jax.experimental.pallas import tpu as pltpu
from jax.sharding import PartitionSpec as P

DL = 32

courant = 0.5
grad_scale = 0.125

MESH = pl.DeviceIdType.MESH
f32 = jnp.float32
bf16 = jnp.bfloat16
LANES = 128
BLOCK = 8


def iota(shape, axis):
    return lax.broadcasted_iota(jnp.int32, shape, axis)


def dot(a, b):
    return jnp.dot(a, b, preferred_element_type=f32)


def one_hot(mask):
    return jnp.where(mask, 1.0, 0.0).astype(bf16)


def hot_rows(count, row):
    size = row.shape[1]
    number = iota((count, size), 0).astype(jnp.int16).reshape(count // 16, 16, size)
    entry = jnp.broadcast_to(row, (16, size)).astype(jnp.int16)
    hot = jnp.where(number == entry[None], jnp.ones((), bf16), jnp.zeros((), bf16))
    return hot.reshape(count, size)


def split(value):
    high = value.astype(bf16)
    return high, (value - high.astype(f32)).astype(bf16)


def next_z(field):
    size = field.shape[1]
    return jnp.where(iota((1, size), 1) == size - 1, 0.0, pltpu.roll(field, size - 1, 1))


def prior_z(field):
    return jnp.where(iota((1, field.shape[1]), 1) == 0, 0.0, pltpu.roll(field, 1, 1))


def next_row(field, edge):
    size = field.shape[0]
    return jnp.where(iota((size, 1), 0) == size - 1, edge, pltpu.roll(field, size - 1, 0))


def prior_row(field, edge):
    return jnp.where(iota((field.shape[0], 1), 0) == 0, edge, pltpu.roll(field, 1, 0))


def exchange(
    count_x,
    count_y,
    e_hbm,
    h_hbm,
    m_hbm,
    eps_hbm,
    f_hbm,
    cs_hbm,
    tp_hbm,
    pr_hbm,
    ne,
    nh,
    recv,
    e_v,
    m_v,
    hy_edge,
    h_v,
    f_v,
    eps_v,
    cs_v,
    tp_v,
    pr_v,
    rt_v,
    acc,
    stage,
    out_y_prev,
    out_y_next,
    in_xn,
    in_xpe,
    in_xph,
    in_yn,
    in_yp,
    in_c1,
    in_c2,
    yn,
    send,
    load_sem,
    face_send,
    face_recv,
    part_send,
    part_recv,
):
    _, cx, cy, nz = e_hbm.shape
    slots = tp_hbm.shape[2]
    devices = count_x * count_y
    half_x, half_y = cx // 2, cy // 2
    width = count_y * half_y
    rank_rows = pr_v.shape[0]
    per_device = slots // devices
    groups = LANES // DL
    rows = per_device // groups
    owned = pr_hbm.shape[0] * LANES // devices

    gx, gy = lax.axis_index("gx"), lax.axis_index("gy")
    me = gx * count_y + gy

    loads = [
        pltpu.make_async_copy(src, dst, load_sem.at[i])
        for i, (src, dst) in enumerate(
            [
                (tp_hbm.at[gx], tp_v),
                (pr_hbm.at[pl.ds(pl.multiple_of(gx * rank_rows, 8), rank_rows)], pr_v),
                (e_hbm, e_v.at[:, pl.ds(0, cx)]),
                (h_hbm, h_v),
                (cs_hbm, cs_v),
                (f_hbm, f_v),
                (eps_hbm, eps_v),
                (m_hbm, m_v),
            ]
        )
    ]
    for load in loads:
        load.start()

    barrier = pltpu.get_barrier_semaphore()

    def partner(step):
        device = lax.rem(me + step, devices)
        return device, (lax.div(device, count_y), lax.rem(device, count_y))

    def each_partner(act):
        main = (devices - 1) // 4 * 4
        lax.fori_loop(1, 1 + main, act, 0, unroll=4)
        for step in range(1 + main, devices):
            act(step, 0)

    def greet(step, carry):
        pl.semaphore_signal(barrier, inc=1, device_id=partner(step)[1], device_id_type=MESH)
        return carry

    each_partner(greet)

    loads[0].wait()
    loads[1].wait()
    tile_row = iota(tp_v.shape, 0) == gy
    ids = jnp.sum(jnp.where(tile_row, tp_v[...], 0), axis=0, keepdims=True)
    listed = ids >= 0
    local = jnp.where(listed, ids - gx * (half_x * width), 0)
    local_row, local_lane = lax.div(local, LANES), lax.rem(local, LANES)
    ranks = pr_v[...]
    if rank_rows < LANES:
        ranks = jnp.concatenate(
            [ranks, jnp.zeros((LANES - rank_rows, LANES), jnp.int32)], axis=0
        )
    turned_high = lax.shift_right_logical(ranks, 8).astype(f32).T
    turned_low = lax.bitwise_and(ranks, 255).astype(f32).T
    table = jnp.concatenate([turned_high.astype(bf16), turned_low.astype(bf16)], axis=0)
    picked = dot(table, one_hot(iota((LANES, slots), 0) == local_row))
    picked = 256.0 * picked[:LANES] + picked[LANES:]
    slot_rank = jnp.sum(
        jnp.where(iota((LANES, slots), 0) == local_lane, picked, 0.0), axis=0, keepdims=True
    )
    turned = 256.0 * turned_high + turned_low
    along_y = lax.rem(iota((LANES, LANES), 1) * LANES + iota((LANES, LANES), 0), width)
    rt_v[...] = jnp.where(lax.div(along_y, half_y) == gy, turned, 1e9)
    tile_ranks = rt_v[
        pl.ds(pl.multiple_of(lax.rem(gy * half_y, LANES), half_y), half_y), :
    ]
    below = jnp.zeros((half_y, slots), f32)
    for j in range(rank_rows):
        below = below + jnp.where(tile_ranks[:, j : j + 1] < slot_rank, 1.0, 0.0)
    place = jnp.sum(below, axis=0, keepdims=True).astype(jnp.int32)
    owner, nth = lax.div(place, per_device), lax.rem(place, per_device)
    line = lax.div(nth, rows) * LANES + lax.rem(nth, rows) * devices + owner
    line = jnp.where(listed, line, -1)
    order = hot_rows(slots, line)
    own_rank = lax.rem(slot_rank.astype(jnp.int32), owned)
    own_high = lax.shift_right_logical(own_rank, 8).astype(f32)
    own_low = lax.bitwise_and(own_rank, 255).astype(f32)
    rank_table = jnp.concatenate(
        [jnp.broadcast_to(own, (LANES, slots)).astype(bf16) for own in (own_high, own_low)],
        axis=0,
    )
    rank_lines = lax.dot_general(
        order, rank_table, (((1,), (1,)), ((), ())), preferred_element_type=f32
    )
    rank_lines = 256.0 * rank_lines[:, :LANES] + rank_lines[:, LANES:]
    lane = iota((devices, LANES), 1)
    rank_block = jnp.zeros((devices, LANES), f32)
    for k in range(per_device):
        part = rank_lines[k * devices : (k + 1) * devices]
        rank_block = jnp.where(lane == k, part, rank_block)

    loads[2].wait()
    loads[4].wait()
    loads[5].wait()
    batch = 256 // cy

    def add_cells(g, carry):
        slot_parts, parts = [], []
        for a in range(batch):
            x = g * batch + a
            slot_parts.append(cs_v[pl.ds(x, 1), :])
            density = e_v[0, x].astype(f32) * f_v[0, x].astype(f32)
            for c in (1, 2):
                density = density + e_v[c, x].astype(f32) * f_v[c, x].astype(f32)
            parts.append(jnp.concatenate(split(density), axis=1))
        cell_slots = jnp.concatenate(slot_parts, axis=1)
        hot = hot_rows(slots, cell_slots)
        acc[...] += dot(hot, jnp.concatenate(parts, axis=0))
        return carry

    acc[...] = jnp.zeros_like(acc)
    lax.fori_loop(0, cx // batch, add_cells, 0, unroll=4)
    loads[3].wait()

    def gather_rows(x, carry):
        for c in range(3):
            first = e_v[c, x, 0:16, :].astype(f32)
            last = e_v[c, x, cy - 16 : cy, :].astype(f32)
            stage[c, pl.ds(x, 1), :] = first[0:1]
            stage[3 + c, pl.ds(x, 1), :] = last[15:16]
        for k, c in enumerate((0, 2)):
            stage[6 + k, pl.ds(x, 1), :] = h_v[c, x, cy - 16 : cy, :].astype(f32)[15:16]
        return carry

    lax.fori_loop(0, cx, gather_rows, 0, unroll=4)
    out_y_prev[0] = stage[0].astype(bf16)
    out_y_prev[1] = stage[2].astype(bf16)
    for k in range(5):
        out_y_next[k] = stage[3 + k].astype(bf16)

    pl.semaphore_wait(barrier, devices - 1)

    faces = [
        (out_y_prev, in_yn, 0, -1),
        (out_y_next, in_yp, 0, 1),
        (e_hbm.at[1, 0, pl.ds(cy - 16, 16)], in_c2, -1, 1),
        (e_hbm.at[pl.ds(1, 2), 0], in_xn, -1, 0),
        (e_hbm.at[:, cx - 1], in_xpe, 1, 0),
        (h_hbm.at[pl.ds(1, 2), cx - 1], in_xph, 1, 0),
        (e_hbm.at[0, cx - 1, pl.ds(0, 16)], in_c1, 1, -1),
    ]

    def inside(step_x, step_y):
        there = None
        for at, step, count in ((gx, step_x, count_x), (gy, step_y, count_y)):
            if step:
                fits = at + step < count if step > 0 else at + step >= 0
                there = fits if there is None else jnp.logical_and(there, fits)
        return there

    def face_copy(i):
        source, landing, step_x, step_y = faces[i]
        return pltpu.make_async_remote_copy(
            src_ref=source,
            dst_ref=landing,
            send_sem=face_send.at[i],
            recv_sem=face_recv.at[i],
            device_id=(gx + step_x, gy + step_y),
            device_id_type=MESH,
        )

    for i, (_, landing, step_x, step_y) in enumerate(faces):

        @pl.when(inside(step_x, step_y))
        def _():
            face_copy(i).start()

        @pl.when(jnp.logical_not(inside(-step_x, -step_y)))
        def _():
            landing[...] = jnp.zeros(landing.shape, landing.dtype)

    sums = acc[:, :nz] + acc[:, nz:]
    sorted_sums = dot(order, jnp.concatenate(split(sums), axis=1)).astype(bf16)
    packed = jnp.concatenate(
        [
            jnp.concatenate(
                [
                    sorted_sums[j * LANES : (j + 1) * LANES, half * nz : (half + 1) * nz]
                    for j in range(groups)
                ],
                axis=1,
            )
            for half in range(2)
        ],
        axis=0,
    )
    layer = lax.div(iota((nz, LANES), 0), nz // DL)
    lane = iota((nz, LANES), 1)
    pool = jnp.concatenate([one_hot(layer + j * DL == lane) for j in range(groups)], axis=0)
    pooled = dot(packed, pool)
    pooled = pooled[:LANES] + pooled[LANES:]
    for i in range(rows):
        part = slice(i * devices, (i + 1) * devices)
        send[pl.ds(i, devices, stride=BLOCK), :] = pooled[part]
    send[pl.ds(rows, devices, stride=BLOCK), :] = rank_block

    used = rows + 1
    mine = pl.ds(pl.multiple_of(me * BLOCK, BLOCK), used)

    def send_part(step, carry):
        device, where = partner(step)
        pltpu.make_async_remote_copy(
            src_ref=send.at[pl.ds(pl.multiple_of(device * BLOCK, BLOCK), used)],
            dst_ref=recv.at[mine],
            send_sem=part_send,
            recv_sem=part_recv,
            device_id=where,
            device_id_type=MESH,
        ).start()
        return carry

    each_partner(send_part)
    recv[mine, :] = send[mine, :]

    def await_faces(which):
        for i in which:

            @pl.when(inside(-faces[i][2], -faces[i][3]))
            def _():
                face_copy(i).wait_recv()

    await_faces([0])
    for k in range(2):
        yn[k] = in_yn[k].astype(f32)

    def update_h(x, carry):
        e_x, e_y, e_z = [e_v[c, x].astype(f32) for c in range(3)]
        nx_y, nx_z = [e_v[c, x + 1].astype(f32) for c in (1, 2)]
        ny_x, ny_z = [yn[k, pl.ds(x, 1), :] for k in range(2)]
        d_y_z, d_z_y = next_row(e_z, ny_z) - e_z, next_z(e_y) - e_y
        nh[0, x] = (h_v[0, x].astype(f32) - courant * (d_y_z - d_z_y)).astype(bf16)
        d_z_x, d_x_z = next_z(e_x) - e_x, nx_z - e_z
        nh[1, x] = (h_v[1, x].astype(f32) - courant * (d_z_x - d_x_z)).astype(bf16)
        d_x_y, d_y_x = nx_y - e_y, next_row(e_x, ny_x) - e_x
        nh[2, x] = (h_v[2, x].astype(f32) - courant * (d_x_y - d_y_x)).astype(bf16)
        return carry

    unrolled = 4
    main = (cx - 1) // unrolled * unrolled
    lax.fori_loop(0, main, update_h, 0, unroll=unrolled)
    for x in range(main, cx - 1):
        update_h(x, 0)
    await_faces([3])
    for c in (1, 2):
        e_v[c, cx] = in_xn[c - 1]
    update_h(cx - 1, 0)

    await_faces([1, 2])
    pe_x, pe_y, pe_z, ph_x, ph_z = [in_yp[k].astype(f32) for k in range(5)]
    first_x, first_z = stage[0], stage[2]
    edge_x = ph_x - courant * ((first_z - pe_z) - (next_z(pe_y) - pe_y))
    corner = in_c2[...].astype(f32)[15:16]
    edge_z = ph_z - courant * ((next_row(pe_y, corner) - pe_y) - (first_x - pe_x))
    keep_y = gy > 0
    hy_edge[0] = jnp.where(keep_y, edge_x, 0.0).astype(bf16).astype(f32)
    hy_edge[1] = jnp.where(keep_y, edge_z, 0.0).astype(bf16).astype(f32)

    loads[6].wait()
    loads[7].wait()
    materials = eps_v.shape[0]
    factors = [courant * eps_v[k] for k in range(materials)]

    def update_e(x, carry):
        back_y, back_z = [value.astype(f32) for value in carry]
        ahead = nh[1, x], nh[2, x]
        h_x = nh[0, x].astype(f32)
        h_y, h_z = [value.astype(f32) for value in ahead]
        before_x, before_z = [hy_edge[k, pl.ds(x, 1), :] for k in range(2)]
        material = m_v[x]
        factor = jnp.full(material.shape, factors[-1], f32)
        for which in range(materials - 1):
            factor = jnp.where(material == which, factors[which], factor)
        b_y_z, b_z_y = h_z - prior_row(h_z, before_z), h_y - prior_z(h_y)
        ne[0, x] = (e_v[0, x].astype(f32) + factor * (b_y_z - b_z_y)).astype(bf16)
        b_z_x, b_x_z = h_x - prior_z(h_x), h_z - back_z
        ne[1, x] = (e_v[1, x].astype(f32) + factor * (b_z_x - b_x_z)).astype(bf16)
        b_x_y, b_y_x = h_y - back_y, h_x - prior_row(h_x, before_x)
        ne[2, x] = (e_v[2, x].astype(f32) + factor * (b_x_y - b_y_x)).astype(bf16)
        return ahead

    carry = nh[1, 0], nh[2, 0]
    carry = lax.fori_loop(1, 1 + main, update_e, carry, unroll=unrolled)
    for x in range(1 + main, cx):
        carry = update_e(x, carry)

    await_faces([4, 5, 6])
    pe_x, pe_y, pe_z = [in_xpe[k].astype(f32) for k in range(3)]
    ph_y, ph_z = [in_xph[k].astype(f32) for k in range(2)]
    first_y, first_z = e_v[1, 0].astype(f32), e_v[2, 0].astype(f32)
    back_y = ph_y - courant * ((next_z(pe_x) - pe_x) - (first_z - pe_z))
    corner = in_c1[...].astype(f32)[0:1]
    back_z = ph_z - courant * ((first_y - pe_y) - (next_row(pe_x, corner) - pe_x))
    keep_x = gx > 0
    edge_y = jnp.where(keep_x, back_y, 0.0).astype(bf16)
    edge_z = jnp.where(keep_x, back_z, 0.0).astype(bf16)

    update_e(0, (edge_y, edge_z))

    others = pl.ds(0, (devices - 1) * used)
    arrivals = pltpu.make_async_remote_copy(
        src_ref=send.at[others],
        dst_ref=recv.at[others],
        send_sem=part_send,
        recv_sem=part_recv,
        device_id=(gx, gy),
        device_id_type=MESH,
    )
    arrivals.wait_recv()
    arrivals.wait_send()
    for i, (_, _, step_x, step_y) in enumerate(faces):

        @pl.when(inside(step_x, step_y))
        def _():
            face_copy(i).wait_send()


def finish(
    ne_v,
    nh_v,
    recv,
    ne,
    nh,
    grad,
    grad_v,
    store_sem,
):
    devices = recv.shape[0] // BLOCK
    owned = grad.shape[1]
    groups = LANES // DL
    rows = owned // devices // groups

    stores = [
        pltpu.make_async_copy(src, dst, store_sem.at[i])
        for i, (src, dst) in enumerate([(ne_v, ne), (nh_v, nh), (grad_v, grad)])
    ]
    stores[0].start()
    stores[1].start()

    values = jnp.concatenate(
        [recv[pl.ds(i, devices, stride=BLOCK), :] for i in range(rows)], axis=0
    )
    value_ranks = recv[pl.ds(rows, devices, stride=BLOCK), :]
    turned_values = values.T
    terms = jnp.concatenate(
        [turned_values[j * DL : (j + 1) * DL] for j in range(groups)], axis=1
    )
    lane_rank = iota((devices, owned), 1).astype(f32)
    target = jnp.concatenate(
        [one_hot(value_ranks[:, k : k + 1] == lane_rank) for k in range(groups * rows)],
        axis=0,
    )
    result = dot(jnp.concatenate(split(terms), axis=0), target)
    grad_v[...] = grad_scale * (result[:DL] + result[DL:])

    stores[2].start()
    for store in stores:
        store.wait()


def per_device(
    adjoint_e, adjoint_h, material, inv_eps, forward_design, cell_slot, tile_pillars, pillar_rank
):
    count_x, count_y = lax.axis_size("gx"), lax.axis_size("gy")
    devices = count_x * count_y
    _, cx, cy, nz = adjoint_e.shape
    slots = tile_pillars.shape[2]
    ranks = pillar_rank.reshape(-1, LANES)
    rank_rows = ranks.shape[0] // count_x
    owned = pillar_rank.shape[0] // devices
    anywhere = pl.BlockSpec(memory_space=pl.ANY)
    vmem = pl.BlockSpec(memory_space=pltpu.VMEM)
    operands = [
        pltpu.with_memory_space_constraint(operand, pltpu.HBM)
        for operand in (
            adjoint_e,
            adjoint_h,
            material,
            inv_eps,
            forward_design,
            cell_slot,
            tile_pillars,
            ranks,
        )
    ]
    kept = pl.pallas_call(
        functools.partial(exchange, count_x, count_y),
        out_shape=(
            pltpu.VMEM((3, cx, cy, nz), bf16),
            pltpu.VMEM((3, cx, cy, nz), bf16),
            pltpu.VMEM((devices * BLOCK, LANES), f32),
        ),
        in_specs=[anywhere] * 8,
        out_specs=(vmem,) * 3,
        scratch_shapes=[
            pltpu.VMEM((3, cx + 1, cy, nz), bf16),
            pltpu.VMEM((cx, cy, nz), jnp.int32),
            pltpu.VMEM((2, cx, nz), f32),
            pltpu.VMEM((3, cx, cy, nz), bf16),
            pltpu.VMEM((3, cx, cy, nz), bf16),
            pltpu.SMEM(inv_eps.shape, f32),
            pltpu.VMEM((cx, cy), jnp.int32),
            pltpu.VMEM((count_y, slots), jnp.int32),
            pltpu.VMEM((rank_rows, LANES), jnp.int32),
            pltpu.VMEM((LANES, LANES), f32),
            pltpu.VMEM((slots, 2 * nz), f32),
            pltpu.VMEM((8, cx, nz), f32),
            pltpu.VMEM((2, cx, nz), bf16),
            pltpu.VMEM((5, cx, nz), bf16),
            pltpu.VMEM((2, cy, nz), bf16),
            pltpu.VMEM((3, cy, nz), bf16),
            pltpu.VMEM((2, cy, nz), bf16),
            pltpu.VMEM((2, cx, nz), bf16),
            pltpu.VMEM((5, cx, nz), bf16),
            pltpu.VMEM((16, nz), bf16),
            pltpu.VMEM((16, nz), bf16),
            pltpu.VMEM((2, cx, nz), f32),
            pltpu.VMEM((devices * BLOCK, LANES), f32),
            pltpu.SemaphoreType.DMA((8,)),
            pltpu.SemaphoreType.DMA((7,)),
            pltpu.SemaphoreType.DMA((7,)),
            pltpu.SemaphoreType.DMA,
            pltpu.SemaphoreType.DMA,
        ],
        compiler_params=pltpu.CompilerParams(
            collective_id=0, has_side_effects=True, vmem_limit_bytes=24 * 1024 * 1024
        ),
    )(*operands)
    return pl.pallas_call(
        finish,
        out_shape=(
            pltpu.HBM(adjoint_e.shape, bf16),
            pltpu.HBM(adjoint_h.shape, bf16),
            pltpu.HBM((DL, owned), f32),
        ),
        in_specs=[vmem] * 3,
        out_specs=(anywhere,) * 3,
        scratch_shapes=[
            pltpu.VMEM((DL, owned), f32),
            pltpu.SemaphoreType.DMA((3,)),
        ],
        compiler_params=pltpu.CompilerParams(vmem_limit_bytes=16 * 1024 * 1024),
    )(*[pltpu.with_memory_space_constraint(value, pltpu.VMEM) for value in kept])


def solution(mesh):
    return jax.shard_map(
        per_device,
        mesh=mesh,
        in_specs=(
            P(None, "gx", "gy", None),
            P(None, "gx", "gy", None),
            P("gx", "gy", None),
            P(),
            P(None, "gx", "gy", None),
            P("gx", "gy"),
            P(),
            P(),
        ),
        out_specs=(P(None, "gx", "gy", None), P(None, "gx", "gy", None), P(None, ("gx", "gy"))),
        check_vma=False,
    )
```

```python
import functools

import jax
import jax.numpy as jnp
from jax import lax
from jax.experimental import pallas as pl
from jax.experimental.pallas import tpu as pltpu
from jax.sharding import PartitionSpec as P

DL = 32

courant = 0.5
grad_scale = 0.125

MESH = pl.DeviceIdType.MESH
f32 = jnp.float32
bf16 = jnp.bfloat16
LANES = 128
BLOCK = 8


def iota(shape, axis):
    return lax.broadcasted_iota(jnp.int32, shape, axis)


def dot(a, b):
    return jnp.dot(a, b, preferred_element_type=f32)


def one_hot(mask):
    return jnp.where(mask, 1.0, 0.0).astype(bf16)


def hot_rows(count, row):
    size = row.shape[1]
    number = iota((count, size), 0).astype(jnp.int16).reshape(count // 16, 16, size)
    entry = jnp.broadcast_to(row, (16, size)).astype(jnp.int16)
    hot = jnp.where(number == entry[None], jnp.ones((), bf16), jnp.zeros((), bf16))
    return hot.reshape(count, size)


def split(value):
    high = value.astype(bf16)
    return high, (value - high.astype(f32)).astype(bf16)


def next_z(field):
    size = field.shape[1]
    return jnp.where(iota((1, size), 1) == size - 1, 0.0, pltpu.roll(field, size - 1, 1))


def prior_z(field):
    return jnp.where(iota((1, field.shape[1]), 1) == 0, 0.0, pltpu.roll(field, 1, 1))


def next_row(field, edge):
    size = field.shape[0]
    return jnp.where(iota((size, 1), 0) == size - 1, edge, pltpu.roll(field, size - 1, 0))


def prior_row(field, edge):
    return jnp.where(iota((field.shape[0], 1), 0) == 0, edge, pltpu.roll(field, 1, 0))


def exchange(
    count_x,
    count_y,
    e_hbm,
    h_hbm,
    m_hbm,
    eps_hbm,
    f_hbm,
    cs_hbm,
    tp_hbm,
    pr_hbm,
    ne,
    nh,
    recv,
    e_v,
    m_v,
    hy_edge,
    h_v,
    f_v,
    eps_v,
    cs_v,
    tp_v,
    pr_v,
    rt_v,
    acc,
    stage,
    out_y_prev,
    out_y_next,
    in_xn,
    in_xpe,
    in_xph,
    in_yn,
    in_yp,
    in_c1,
    in_c2,
    yn,
    send,
    load_sem,
    face_send,
    face_recv,
    part_send,
    part_recv,
):
    _, cx, cy, nz = e_hbm.shape
    slots = tp_hbm.shape[2]
    devices = count_x * count_y
    half_x, half_y = cx // 2, cy // 2
    width = count_y * half_y
    rank_rows = pr_v.shape[0]
    per_device = slots // devices
    groups = LANES // DL
    rows = per_device // groups
    owned = pr_hbm.shape[0] * LANES // devices

    gx, gy = lax.axis_index("gx"), lax.axis_index("gy")
    me = gx * count_y + gy

    def field(src, dst):
        return [(src.at[c], dst.at[c, pl.ds(0, cx)]) for c in range(3)]

    my_ranks = pr_hbm.at[pl.ds(pl.multiple_of(gx * rank_rows, 8), rank_rows)]
    sources = [
        [(tp_hbm.at[gx], tp_v)],
        [(my_ranks, pr_v)],
        field(e_hbm, e_v),
        field(h_hbm, h_v),
        [(cs_hbm, cs_v)],
        field(f_hbm, f_v),
        [(eps_hbm, eps_v)],
        [(m_hbm, m_v)],
    ]
    loads = [
        [
            pltpu.make_async_copy(src, dst, load_sem.at[3 * i + c])
            for c, (src, dst) in enumerate(group)
        ]
        for i, group in enumerate(sources)
    ]
    for i in (0, 1, 4, 2, 5, 3, 6, 7):
        for load in loads[i]:
            load.start()

    def await_load(i):
        for load in loads[i]:
            load.wait()

    barrier = pltpu.get_barrier_semaphore()

    def partner(step):
        device = lax.rem(me + step, devices)
        return device, (lax.div(device, count_y), lax.rem(device, count_y))

    def each_partner(act):
        main = (devices - 1) // 4 * 4
        lax.fori_loop(1, 1 + main, act, 0, unroll=4)
        for step in range(1 + main, devices):
            act(step, 0)

    def greet(step, carry):
        pl.semaphore_signal(barrier, inc=1, device_id=partner(step)[1], device_id_type=MESH)
        return carry

    each_partner(greet)

    await_load(0)
    await_load(1)
    tile_row = iota(tp_v.shape, 0) == gy
    ids = jnp.sum(jnp.where(tile_row, tp_v[...], 0), axis=0, keepdims=True)
    listed = ids >= 0
    local = jnp.where(listed, ids - gx * (half_x * width), 0)
    local_row, local_lane = lax.div(local, LANES), lax.rem(local, LANES)
    ranks = pr_v[...]
    if rank_rows < LANES:
        ranks = jnp.concatenate(
            [ranks, jnp.zeros((LANES - rank_rows, LANES), jnp.int32)], axis=0
        )
    turned_high = lax.shift_right_logical(ranks, 8).astype(f32).T
    turned_low = lax.bitwise_and(ranks, 255).astype(f32).T
    table = jnp.concatenate([turned_high.astype(bf16), turned_low.astype(bf16)], axis=0)
    picked = dot(table, one_hot(iota((LANES, slots), 0) == local_row))
    picked = 256.0 * picked[:LANES] + picked[LANES:]
    slot_rank = jnp.sum(
        jnp.where(iota((LANES, slots), 0) == local_lane, picked, 0.0), axis=0, keepdims=True
    )
    turned = 256.0 * turned_high + turned_low
    along_y = lax.rem(iota((LANES, LANES), 1) * LANES + iota((LANES, LANES), 0), width)
    rt_v[...] = jnp.where(lax.div(along_y, half_y) == gy, turned, 1e9)
    tile_ranks = rt_v[
        pl.ds(pl.multiple_of(lax.rem(gy * half_y, LANES), half_y), half_y), :
    ]
    below = jnp.zeros((half_y, slots), f32)
    for j in range(rank_rows):
        below = below + jnp.where(tile_ranks[:, j : j + 1] < slot_rank, 1.0, 0.0)
    place = jnp.sum(below, axis=0, keepdims=True).astype(jnp.int32)
    owner, nth = lax.div(place, per_device), lax.rem(place, per_device)
    line = lax.div(nth, rows) * LANES + lax.rem(nth, rows) * devices + owner
    line = jnp.where(listed, line, -1)
    order = hot_rows(slots, line)
    own_rank = lax.rem(slot_rank.astype(jnp.int32), owned)
    own_high = lax.shift_right_logical(own_rank, 8).astype(f32)
    own_low = lax.bitwise_and(own_rank, 255).astype(f32)
    rank_table = jnp.concatenate(
        [jnp.broadcast_to(own, (LANES, slots)).astype(bf16) for own in (own_high, own_low)],
        axis=0,
    )
    rank_lines = lax.dot_general(
        order, rank_table, (((1,), (1,)), ((), ())), preferred_element_type=f32
    )
    rank_lines = 256.0 * rank_lines[:, :LANES] + rank_lines[:, LANES:]
    lane = iota((devices, LANES), 1)
    rank_block = jnp.zeros((devices, LANES), f32)
    for k in range(per_device):
        part = rank_lines[k * devices : (k + 1) * devices]
        rank_block = jnp.where(lane == k, part, rank_block)

    await_load(2)
    await_load(4)
    await_load(5)
    batch = 256 // cy

    def add_cells(g, carry):
        slot_parts, parts = [], []
        for a in range(batch):
            x = g * batch + a
            slot_parts.append(cs_v[pl.ds(x, 1), :])
            density = e_v[0, x].astype(f32) * f_v[0, x].astype(f32)
            for c in (1, 2):
                density = density + e_v[c, x].astype(f32) * f_v[c, x].astype(f32)
            parts.append(jnp.concatenate(split(density), axis=1))
        cell_slots = jnp.concatenate(slot_parts, axis=1)
        hot = hot_rows(slots, cell_slots)
        acc[...] += dot(hot, jnp.concatenate(parts, axis=0))
        return carry

    acc[...] = jnp.zeros_like(acc)
    lax.fori_loop(0, cx // batch, add_cells, 0, unroll=4)
    await_load(3)

    def gather_rows(x, carry):
        for c in range(3):
            first = e_v[c, x, 0:16, :].astype(f32)
            last = e_v[c, x, cy - 16 : cy, :].astype(f32)
            stage[c, pl.ds(x, 1), :] = first[0:1]
            stage[3 + c, pl.ds(x, 1), :] = last[15:16]
        for k, c in enumerate((0, 2)):
            stage[6 + k, pl.ds(x, 1), :] = h_v[c, x, cy - 16 : cy, :].astype(f32)[15:16]
        return carry

    lax.fori_loop(0, cx, gather_rows, 0, unroll=4)
    out_y_prev[0] = stage[0].astype(bf16)
    out_y_prev[1] = stage[2].astype(bf16)
    for k in range(5):
        out_y_next[k] = stage[3 + k].astype(bf16)

    pl.semaphore_wait(barrier, devices - 1)

    faces = [
        (out_y_prev, in_yn, 0, -1),
        (out_y_next, in_yp, 0, 1),
        (e_hbm.at[1, 0, pl.ds(cy - 16, 16)], in_c2, -1, 1),
        (e_hbm.at[pl.ds(1, 2), 0], in_xn, -1, 0),
        (e_hbm.at[:, cx - 1], in_xpe, 1, 0),
        (h_hbm.at[pl.ds(1, 2), cx - 1], in_xph, 1, 0),
        (e_hbm.at[0, cx - 1, pl.ds(0, 16)], in_c1, 1, -1),
    ]

    def inside(step_x, step_y):
        there = None
        for at, step, count in ((gx, step_x, count_x), (gy, step_y, count_y)):
            if step:
                fits = at + step < count if step > 0 else at + step >= 0
                there = fits if there is None else jnp.logical_and(there, fits)
        return there

    def face_copy(i):
        source, landing, step_x, step_y = faces[i]
        return pltpu.make_async_remote_copy(
            src_ref=source,
            dst_ref=landing,
            send_sem=face_send.at[i],
            recv_sem=face_recv.at[i],
            device_id=(gx + step_x, gy + step_y),
            device_id_type=MESH,
        )

    for i, (_, landing, step_x, step_y) in enumerate(faces):

        @pl.when(inside(step_x, step_y))
        def _():
            face_copy(i).start()

        @pl.when(jnp.logical_not(inside(-step_x, -step_y)))
        def _():
            landing[...] = jnp.zeros(landing.shape, landing.dtype)

    sums = acc[:, :nz] + acc[:, nz:]
    sorted_sums = dot(order, jnp.concatenate(split(sums), axis=1)).astype(bf16)
    packed = jnp.concatenate(
        [
            jnp.concatenate(
                [
                    sorted_sums[j * LANES : (j + 1) * LANES, half * nz : (half + 1) * nz]
                    for j in range(groups)
                ],
                axis=1,
            )
            for half in range(2)
        ],
        axis=0,
    )
    layer = lax.div(iota((nz, LANES), 0), nz // DL)
    lane = iota((nz, LANES), 1)
    pool = jnp.concatenate([one_hot(layer + j * DL == lane) for j in range(groups)], axis=0)
    pooled = dot(packed, pool)
    pooled = pooled[:LANES] + pooled[LANES:]
    for i in range(rows):
        part = slice(i * devices, (i + 1) * devices)
        send[pl.ds(i, devices, stride=BLOCK), :] = pooled[part]
    send[pl.ds(rows, devices, stride=BLOCK), :] = rank_block

    used = rows + 1
    mine = pl.ds(pl.multiple_of(me * BLOCK, BLOCK), used)

    def send_part(step, carry):
        device, where = partner(step)
        pltpu.make_async_remote_copy(
            src_ref=send.at[pl.ds(pl.multiple_of(device * BLOCK, BLOCK), used)],
            dst_ref=recv.at[mine],
            send_sem=part_send,
            recv_sem=part_recv,
            device_id=where,
            device_id_type=MESH,
        ).start()
        return carry

    each_partner(send_part)
    recv[mine, :] = send[mine, :]

    def await_faces(which):
        for i in which:

            @pl.when(inside(-faces[i][2], -faces[i][3]))
            def _():
                face_copy(i).wait_recv()

    await_faces([0])
    for k in range(2):
        yn[k] = in_yn[k].astype(f32)

    def update_h(x, carry):
        e_x, e_y, e_z = [e_v[c, x].astype(f32) for c in range(3)]
        nx_y, nx_z = [e_v[c, x + 1].astype(f32) for c in (1, 2)]
        ny_x, ny_z = [yn[k, pl.ds(x, 1), :] for k in range(2)]
        d_y_z, d_z_y = next_row(e_z, ny_z) - e_z, next_z(e_y) - e_y
        nh[0, x] = (h_v[0, x].astype(f32) - courant * (d_y_z - d_z_y)).astype(bf16)
        d_z_x, d_x_z = next_z(e_x) - e_x, nx_z - e_z
        nh[1, x] = (h_v[1, x].astype(f32) - courant * (d_z_x - d_x_z)).astype(bf16)
        d_x_y, d_y_x = nx_y - e_y, next_row(e_x, ny_x) - e_x
        nh[2, x] = (h_v[2, x].astype(f32) - courant * (d_x_y - d_y_x)).astype(bf16)
        return carry

    unrolled = 4
    main = (cx - 1) // unrolled * unrolled
    lax.fori_loop(0, main, update_h, 0, unroll=unrolled)
    for x in range(main, cx - 1):
        update_h(x, 0)
    await_faces([3])
    for c in (1, 2):
        e_v[c, cx] = in_xn[c - 1]
    update_h(cx - 1, 0)

    await_faces([1, 2])
    pe_x, pe_y, pe_z, ph_x, ph_z = [in_yp[k].astype(f32) for k in range(5)]
    first_x, first_z = stage[0], stage[2]
    edge_x = ph_x - courant * ((first_z - pe_z) - (next_z(pe_y) - pe_y))
    corner = in_c2[...].astype(f32)[15:16]
    edge_z = ph_z - courant * ((next_row(pe_y, corner) - pe_y) - (first_x - pe_x))
    keep_y = gy > 0
    hy_edge[0] = jnp.where(keep_y, edge_x, 0.0).astype(bf16).astype(f32)
    hy_edge[1] = jnp.where(keep_y, edge_z, 0.0).astype(bf16).astype(f32)

    await_load(6)
    await_load(7)
    materials = eps_v.shape[0]
    factors = [courant * eps_v[k] for k in range(materials)]

    def update_e(x, carry):
        back_y, back_z = [value.astype(f32) for value in carry]
        ahead = nh[1, x], nh[2, x]
        h_x = nh[0, x].astype(f32)
        h_y, h_z = [value.astype(f32) for value in ahead]
        before_x, before_z = [hy_edge[k, pl.ds(x, 1), :] for k in range(2)]
        material = m_v[x]
        factor = jnp.full(material.shape, factors[-1], f32)
        for which in range(materials - 1):
            factor = jnp.where(material == which, factors[which], factor)
        b_y_z, b_z_y = h_z - prior_row(h_z, before_z), h_y - prior_z(h_y)
        ne[0, x] = (e_v[0, x].astype(f32) + factor * (b_y_z - b_z_y)).astype(bf16)
        b_z_x, b_x_z = h_x - prior_z(h_x), h_z - back_z
        ne[1, x] = (e_v[1, x].astype(f32) + factor * (b_z_x - b_x_z)).astype(bf16)
        b_x_y, b_y_x = h_y - back_y, h_x - prior_row(h_x, before_x)
        ne[2, x] = (e_v[2, x].astype(f32) + factor * (b_x_y - b_y_x)).astype(bf16)
        return ahead

    carry = nh[1, 0], nh[2, 0]
    carry = lax.fori_loop(1, 1 + main, update_e, carry, unroll=unrolled)
    for x in range(1 + main, cx):
        carry = update_e(x, carry)

    await_faces([4, 5, 6])
    pe_x, pe_y, pe_z = [in_xpe[k].astype(f32) for k in range(3)]
    ph_y, ph_z = [in_xph[k].astype(f32) for k in range(2)]
    first_y, first_z = e_v[1, 0].astype(f32), e_v[2, 0].astype(f32)
    back_y = ph_y - courant * ((next_z(pe_x) - pe_x) - (first_z - pe_z))
    corner = in_c1[...].astype(f32)[0:1]
    back_z = ph_z - courant * ((first_y - pe_y) - (next_row(pe_x, corner) - pe_x))
    keep_x = gx > 0
    edge_y = jnp.where(keep_x, back_y, 0.0).astype(bf16)
    edge_z = jnp.where(keep_x, back_z, 0.0).astype(bf16)

    update_e(0, (edge_y, edge_z))

    others = pl.ds(0, (devices - 1) * used)
    arrivals = pltpu.make_async_remote_copy(
        src_ref=send.at[others],
        dst_ref=recv.at[others],
        send_sem=part_send,
        recv_sem=part_recv,
        device_id=(gx, gy),
        device_id_type=MESH,
    )
    arrivals.wait_recv()
    arrivals.wait_send()
    for i, (_, _, step_x, step_y) in enumerate(faces):

        @pl.when(inside(step_x, step_y))
        def _():
            face_copy(i).wait_send()


def finish(
    ne_v,
    nh_v,
    recv,
    ne,
    nh,
    grad,
    grad_v,
    store_sem,
):
    devices = recv.shape[0] // BLOCK
    owned = grad.shape[1]
    groups = LANES // DL
    rows = owned // devices // groups

    pairs = [(src.at[c], dst.at[c]) for src, dst in ((ne_v, ne), (nh_v, nh)) for c in range(3)]
    stores = [
        pltpu.make_async_copy(src, dst, store_sem.at[i])
        for i, (src, dst) in enumerate(pairs + [(grad_v, grad)])
    ]
    for store in stores[:-1]:
        store.start()

    values = jnp.concatenate(
        [recv[pl.ds(i, devices, stride=BLOCK), :] for i in range(rows)], axis=0
    )
    value_ranks = recv[pl.ds(rows, devices, stride=BLOCK), :]
    turned_values = values.T
    terms = jnp.concatenate(
        [turned_values[j * DL : (j + 1) * DL] for j in range(groups)], axis=1
    )
    lane_rank = iota((devices, owned), 1).astype(f32)
    target = jnp.concatenate(
        [one_hot(value_ranks[:, k : k + 1] == lane_rank) for k in range(groups * rows)],
        axis=0,
    )
    result = dot(jnp.concatenate(split(terms), axis=0), target)
    grad_v[...] = grad_scale * (result[:DL] + result[DL:])

    stores[-1].start()
    for store in stores:
        store.wait()


def per_device(
    adjoint_e, adjoint_h, material, inv_eps, forward_design, cell_slot, tile_pillars, pillar_rank
):
    count_x, count_y = lax.axis_size("gx"), lax.axis_size("gy")
    devices = count_x * count_y
    _, cx, cy, nz = adjoint_e.shape
    slots = tile_pillars.shape[2]
    ranks = pillar_rank.reshape(-1, LANES)
    rank_rows = ranks.shape[0] // count_x
    owned = pillar_rank.shape[0] // devices
    anywhere = pl.BlockSpec(memory_space=pl.ANY)
    vmem = pl.BlockSpec(memory_space=pltpu.VMEM)
    operands = [
        pltpu.with_memory_space_constraint(operand, pltpu.HBM)
        for operand in (
            adjoint_e,
            adjoint_h,
            material,
            inv_eps,
            forward_design,
            cell_slot,
            tile_pillars,
            ranks,
        )
    ]
    kept = pl.pallas_call(
        functools.partial(exchange, count_x, count_y),
        out_shape=(
            pltpu.VMEM((3, cx, cy, nz), bf16),
            pltpu.VMEM((3, cx, cy, nz), bf16),
            pltpu.VMEM((devices * BLOCK, LANES), f32),
        ),
        in_specs=[anywhere] * 8,
        out_specs=(vmem,) * 3,
        scratch_shapes=[
            pltpu.VMEM((3, cx + 1, cy, nz), bf16),
            pltpu.VMEM((cx, cy, nz), jnp.int32),
            pltpu.VMEM((2, cx, nz), f32),
            pltpu.VMEM((3, cx, cy, nz), bf16),
            pltpu.VMEM((3, cx, cy, nz), bf16),
            pltpu.SMEM(inv_eps.shape, f32),
            pltpu.VMEM((cx, cy), jnp.int32),
            pltpu.VMEM((count_y, slots), jnp.int32),
            pltpu.VMEM((rank_rows, LANES), jnp.int32),
            pltpu.VMEM((LANES, LANES), f32),
            pltpu.VMEM((slots, 2 * nz), f32),
            pltpu.VMEM((8, cx, nz), f32),
            pltpu.VMEM((2, cx, nz), bf16),
            pltpu.VMEM((5, cx, nz), bf16),
            pltpu.VMEM((2, cy, nz), bf16),
            pltpu.VMEM((3, cy, nz), bf16),
            pltpu.VMEM((2, cy, nz), bf16),
            pltpu.VMEM((2, cx, nz), bf16),
            pltpu.VMEM((5, cx, nz), bf16),
            pltpu.VMEM((16, nz), bf16),
            pltpu.VMEM((16, nz), bf16),
            pltpu.VMEM((2, cx, nz), f32),
            pltpu.VMEM((devices * BLOCK, LANES), f32),
            pltpu.SemaphoreType.DMA((24,)),
            pltpu.SemaphoreType.DMA((7,)),
            pltpu.SemaphoreType.DMA((7,)),
            pltpu.SemaphoreType.DMA,
            pltpu.SemaphoreType.DMA,
        ],
        compiler_params=pltpu.CompilerParams(
            collective_id=0, has_side_effects=True, vmem_limit_bytes=24 * 1024 * 1024
        ),
    )(*operands)
    return pl.pallas_call(
        finish,
        out_shape=(
            pltpu.HBM(adjoint_e.shape, bf16),
            pltpu.HBM(adjoint_h.shape, bf16),
            pltpu.HBM((DL, owned), f32),
        ),
        in_specs=[vmem] * 3,
        out_specs=(anywhere,) * 3,
        scratch_shapes=[
            pltpu.VMEM((DL, owned), f32),
            pltpu.SemaphoreType.DMA((7,)),
        ],
        compiler_params=pltpu.CompilerParams(vmem_limit_bytes=16 * 1024 * 1024),
    )(*[pltpu.with_memory_space_constraint(value, pltpu.VMEM) for value in kept])


def solution(mesh):
    return jax.shard_map(
        per_device,
        mesh=mesh,
        in_specs=(
            P(None, "gx", "gy", None),
            P(None, "gx", "gy", None),
            P("gx", "gy", None),
            P(),
            P(None, "gx", "gy", None),
            P("gx", "gy"),
            P(),
            P(),
        ),
        out_specs=(P(None, "gx", "gy", None), P(None, "gx", "gy", None), P(None, ("gx", "gy"))),
        check_vma=False,
    )
```
